256 devices in a mesh: seq: 64 (over y, z, core), grp: 4 (over x).
Axes of the slice: x: 4, y: 4, z: 8, core: 2. Of those that a mesh axis runs over, the one named last changes fastest.
Arguments:
- queries: bfloat16 [16384, 8192], P(('grp', 'seq')), parts along dimension 0, may hold values from -6 to 6, as said below
- key_heads: bfloat16 [16384, 1024], P(('grp', 'seq')), parts along dimension 0, may hold values from -6 to 6, as said below
- value_heads: bfloat16 [16384, 1024], P(('grp', 'seq')), parts along dimension 0, may hold values from -6 to 6
- doc_lengths: int32 [32], P('grp'), parts along dimension 0, may hold values from 1 to 1024, 4096 in all
Outputs:
- attended: bfloat16 [16384, 8192], P(('grp', 'seq')), parts along dimension 0
The draws below stay inside these ranges and needn't reach their ends.
There are 4 independent parts, one for each index of `grp`. The reference program is written for one: setup_inputs(seed, part) draws one part's arguments, and reference() takes and returns one part's arrays. A program takes and returns all parts, laid end to end along the dimension named above; each array names one. Nothing has to cross between parts.
Inputs may be any that keep to these rules, and one draw needn't show every extreme that they name: `doc_lengths`: 8 documents, each of 1 to 1024 tokens, together 4096 tokens; one document has exactly 1024 tokens. `queries`: real values. `key_heads`: real values.
All inputs are finite; a program needn't handle non-finite values.
Results may differ from the reference program's by a relative error of at most 0.007.
Values may be sent and summed in bfloat16 or wider, within the bound.
No kernel may reach another device: no remote copies, remote signals or barrier semaphores. Data moves between devices by JAX's collectives and lax.ppermute only.
A program may use at most 128 MiB of HBM per device.

```python
import math
import jax
import jax.numpy as jnp
import numpy as np
from jax import lax

HK = 8
GROUP = 8
DH = 128
TOK_DEV = 64
SPAN = 16
HQ = 64
SEQ = 4096
MAXDOC = 1024
DOCS = 8


def draw_queries(key, part):
    key = jax.random.fold_in(key, 1)
    return jnp.clip(jax.random.normal(key, (SEQ, HQ * DH)), -4.5, 4.5).astype(jnp.bfloat16)


def draw_key_heads(key, part):
    key = jax.random.fold_in(key, 5)
    return jnp.clip(jax.random.normal(key, (SEQ, HK * DH)), -4.5, 4.5).astype(jnp.bfloat16)


def shard_levels(own_key, shape, split, least, largest):
    def one(axis_at, shards_of):
        draws = jax.random.uniform(jax.random.fold_in(jax.random.fold_in(own_key, 6), axis_at), (shards_of,), jnp.float32, least / len(split), largest / len(split))
        return jnp.repeat(jnp.exp(draws), shape[axis_at] // shards_of).reshape((-1,) + (1,) * (len(shape) - axis_at - 1))

    level = one(*split[0])
    for cut in split[1:]:
        level = level * one(*cut)
    return level


def split_up(amount, total, most, lean):
    loads = [(1 << 20) // math.isqrt(standing ** lean) + 1 for standing in range(2, amount + 1)]
    rest, given = total - most - (amount - 1), [1] * (amount - 1)
    while rest > 0:
        movable = [i for i in range(amount - 1) if given[i] < most]
        whole, budget = sum([loads[i] for i in movable]), rest
        for i in movable:
            extra = min(most - given[i], max(1, budget * loads[i] // whole), rest)
            given[i] = given[i] + extra
            rest = rest - extra
    return np.array([most] + given)


def uneven(key, number_of, total, most, lean):
    if number_of == 2:
        one = jax.random.randint(key, (), max(1, total - most), min(most, total - 1) + 1)
        return jnp.stack([one, total - one])
    tallies = jnp.asarray(split_up(number_of, total, most, lean), jnp.int32)
    pairs = (number_of - 1) // 2
    source_of, receiver = tallies[1:1 + 2 * pairs:2], tallies[2:2 + 2 * pairs:2]
    room = jnp.minimum(source_of - 1, most - receiver)
    shifted = jax.random.randint(jax.random.fold_in(key, 1), (pairs,), 0, 1 << 20) % (room + 1)
    tallies = tallies.at[1:1 + 2 * pairs:2].set(source_of - shifted).at[2:2 + 2 * pairs:2].set(receiver + shifted)
    return tallies[jax.random.permutation(jax.random.fold_in(key, 2), number_of)]


def noise(key, shape, deviation, bound, cuts=(), held_as=jnp.bfloat16):
    array = jax.random.normal(key, shape, jnp.float32) * deviation
    if len(cuts) > 0:
        array = shard_levels(key, shape, cuts, -0.22, 0.18) * array
    return jnp.clip(array, min=-bound, max=bound).astype(held_as)


def setup_inputs(seed: int = 0, part: int = 0) -> dict:
    arg_keys = jax.random.split(jax.random.key(seed), 5)
    part_splits = jax.random.split(jax.random.fold_in(arg_keys[4], part), 5)
    return {
        "queries": draw_queries(jax.random.fold_in(jax.random.fold_in(arg_keys[4], part), 71), part),
        "key_heads": draw_key_heads(jax.random.fold_in(jax.random.fold_in(arg_keys[4], part), 71), part),
        "value_heads": noise(part_splits[2], (SEQ, HK * DH), 1.0, 6.0, ((0, 64),)),
        "doc_lengths": uneven(part_splits[3], DOCS, SEQ, MAXDOC, 2).astype(jnp.int32),
    }


def reference(queries, key_heads, value_heads, doc_lengths):
    total_rows = queries.shape[0]
    doc_ends = jnp.cumsum(doc_lengths)
    positions = jnp.arange(total_rows, dtype=jnp.int32)
    segment = jnp.sum((positions[:, None] >= doc_ends[None, :]).astype(jnp.int32), axis=1)
    leading = SPAN * TOK_DEV
    window = leading + TOK_DEV
    key_pad = jnp.pad(key_heads.reshape(total_rows, HK, DH), ((leading, 0), (0, 0), (0, 0)))
    value_pad = jnp.pad(value_heads.reshape(total_rows, HK, DH), ((leading, 0), (0, 0), (0, 0)))
    segment_pad = jnp.pad(segment, (leading, 0), constant_values=-1)
    softmax_scale = DH ** -0.5

    def attend_block(index):
        first_row = (index * TOK_DEV).astype(jnp.int32)
        query_block = lax.dynamic_slice_in_dim(queries, first_row, TOK_DEV, 0).reshape(TOK_DEV, HK, GROUP, DH).astype(jnp.float32)
        key_block = lax.dynamic_slice_in_dim(key_pad, first_row, window, 0).astype(jnp.float32)
        value_block = lax.dynamic_slice_in_dim(value_pad, first_row, window, 0).astype(jnp.float32)
        query_seg = lax.dynamic_slice_in_dim(segment, first_row, TOK_DEV, 0)
        key_seg = lax.dynamic_slice_in_dim(segment_pad, first_row, window, 0)
        query_pos = first_row + jnp.arange(TOK_DEV, dtype=jnp.int32)
        key_pos = first_row - leading + jnp.arange(window, dtype=jnp.int32)
        visible = (query_seg[:, None] == key_seg[None, :]) & (key_pos[None, :] <= query_pos[:, None])
        scores = jnp.einsum("tkgd,skd->kgts", query_block, key_block) * softmax_scale
        scores = jnp.where(visible, scores, -1e30)
        row_max = jnp.max(scores, axis=-1, keepdims=True)
        weights = jnp.where(visible, jnp.exp(scores - row_max), 0.0)
        denom_sum = jnp.sum(weights, axis=-1)
        rounded = lax.optimization_barrier(weights.astype(jnp.bfloat16)).astype(jnp.float32)
        summed = jnp.einsum("kgts,skd->tkgd", rounded, value_block)
        result = summed / jnp.transpose(denom_sum, (2, 0, 1))[..., None]
        return result.reshape(TOK_DEV, HQ * DH).astype(jnp.bfloat16)

    blocks = lax.map(attend_block, jnp.arange(total_rows // TOK_DEV, dtype=jnp.int32))
    return blocks.reshape(total_rows, HQ * DH)
```

```python
import functools

import jax
import jax.numpy as jnp
from jax import lax
from jax.experimental import pallas as pl
from jax.experimental.pallas import tpu as pltpu
from jax.sharding import PartitionSpec as P

HK = 8
GROUP = 8
DH = 128
HQ = 64
ROWS = 64
COLS = GROUP * ROWS
NEG = -1e30
SCALE = DH ** (-0.5)

CHIPS = 32
NEAR = 4
FAR = 8


def chip_route(ahead):
    return [(2 * c + k, 2 * ((c + ahead) % CHIPS) + k) for c in range(CHIPS) for k in range(2)]


SIBLING = [(i, i ^ 1) for i in range(2 * CHIPS)]


def flash_kernel(n_shards, first, last, distances, *refs):
    here_ref, docs_ref, q_ref = refs[:3]
    refs = refs[3:]
    kv = refs[: 2 * n_shards]
    refs = refs[2 * n_shards :]
    if first:
        m_in = l_in = acc_in = None
    else:
        m_in, l_in, acc_in = refs[:3]
        refs = refs[3:]
    if last:
        (out_ref,) = refs
    else:
        m_out, l_out, acc_out = refs

    here = here_ref[0]
    core = lax.rem(here, 2)
    col = lax.broadcasted_iota(jnp.int32, (1, COLS), 1)
    q_pos = here * ROWS + lax.rem(col, ROWS)
    start = jnp.zeros_like(q_pos)
    end = jnp.int32(0)
    for d in range(8):
        end = end + docs_ref[d]
        start = jnp.where(q_pos >= end, end, start)
    n_keys = n_shards * ROWS
    row = lax.broadcasted_iota(jnp.int32, (ROWS, 1), 0)
    k_pos = jnp.concatenate([here_off(here, core, d) * ROWS + row for d in distances], axis=0)
    visible = (k_pos >= start) & (k_pos <= q_pos)

    for h in range(HK):
        cols = slice(h * DH, (h + 1) * DH)
        keys = jnp.concatenate([kv[2 * s][:, cols] for s in range(n_shards)], axis=0)
        values = jnp.concatenate([kv[2 * s + 1][:, cols] for s in range(n_shards)], axis=0)
        q = jnp.concatenate(
            [q_ref[:, (h * GROUP + g) * DH : (h * GROUP + g + 1) * DH] for g in range(GROUP)], axis=0
        )
        scores = lax.dot_general(keys, q, (((1,), (1,)), ((), ())), preferred_element_type=jnp.float32)
        scores = jnp.where(visible, scores * SCALE, NEG)
        top = jnp.max(scores, axis=0, keepdims=True)
        if not first:
            old = m_in[h : h + 1, :]
            top = jnp.maximum(top, old)
        weights = jnp.exp(scores - top)
        total = jnp.sum(weights, axis=0, keepdims=True)
        part = lax.dot_general(
            values, weights.astype(jnp.bfloat16), (((0,), (0,)), ((), ())), preferred_element_type=jnp.float32
        )
        if not first:
            factor = jnp.exp(old - top)
            total = total + l_in[h : h + 1, :] * factor
            part = part + acc_in[h] * factor
        if last:
            result = (part / total).T.astype(jnp.bfloat16)
            for g in range(GROUP):
                out_ref[:, (h * GROUP + g) * DH : (h * GROUP + g + 1) * DH] = result[g * ROWS : (g + 1) * ROWS, :]
        else:
            m_out[h : h + 1, :] = top
            l_out[h : h + 1, :] = total
            acc_out[h] = part


def here_off(here, core, distance):
    chips, sibling = distance
    return here - 2 * chips + (1 - 2 * core if sibling else 0)


def flash(here, docs, q, shards, distances, state, last):
    first = state is None
    n = len(distances)
    vmem = pl.BlockSpec(memory_space=pltpu.VMEM)
    smem = pl.BlockSpec(memory_space=pltpu.SMEM)
    operands = [here, docs, q] + list(shards) + ([] if first else list(state))
    specs = [smem, smem] + [vmem] * (len(operands) - 2)
    if last:
        out_shape = jax.ShapeDtypeStruct((ROWS, HQ * DH), jnp.bfloat16)
        out_specs = vmem
    else:
        out_shape = (
            jax.ShapeDtypeStruct((HK, COLS), jnp.float32),
            jax.ShapeDtypeStruct((HK, COLS), jnp.float32),
            jax.ShapeDtypeStruct((HK, DH, COLS), jnp.float32),
        )
        out_specs = (vmem, vmem, vmem)
    return pl.pallas_call(
        functools.partial(flash_kernel, n, first, last, tuple(distances)),
        out_shape=out_shape,
        in_specs=specs,
        out_specs=out_specs,
        compiler_params=pltpu.CompilerParams(vmem_limit_bytes=48 * 1024 * 1024),
        cost_estimate=pl.CostEstimate(
            flops=4 * n * ROWS * HQ * ROWS * DH, bytes_accessed=2 << 20, transcendentals=n * ROWS * HQ * ROWS
        ),
    )(*operands)


def per_device(queries, key_heads, value_heads, doc_lengths):
    here = lax.axis_index("seq").astype(jnp.int32).reshape(1)

    def send(block, ahead):
        return lax.ppermute(block, "seq", chip_route(ahead))

    def swap(blocks):
        n = len(blocks)
        got = lax.ppermute(jnp.concatenate(blocks, axis=0), "seq", SIBLING)
        return [got[i * ROWS : (i + 1) * ROWS] for i in range(n)]

    own = (key_heads, value_heads)
    near, far = own, own
    shards = [list(own) + swap(own)]
    distances = [[(0, False), (0, True)]]
    for step in range(NEAR):
        near = tuple(send(x, 1) for x in near)
        far = tuple(send(x, FAR if step == 0 else -1) for x in far)
        both = list(near) + list(far)
        shards.append(both + swap(both))
        distances.append([(step + 1, False), (FAR - step, False), (step + 1, True), (FAR - step, True)])

    early = sum(shards[:NEAR], [])
    early_at = sum(distances[:NEAR], [])
    state = flash(here, doc_lengths, queries, early, early_at, None, False)
    return flash(here, doc_lengths, queries, shards[NEAR], distances[NEAR], state, True)


def solution(mesh):
    return jax.shard_map(
        per_device,
        mesh=mesh,
        in_specs=(
            P(("grp", "seq"), None),
            P(("grp", "seq"), None),
            P(("grp", "seq"), None),
            P("grp"),
        ),
        out_specs=P(("grp", "seq"), None),
        check_vma=False,
    )
```

```python
import functools

import jax
import jax.numpy as jnp
from jax import lax
from jax.experimental import pallas as pl
from jax.experimental.pallas import tpu as pltpu
from jax.sharding import PartitionSpec as P

HK = 8
GROUP = 8
DH = 128
HQ = 64
ROWS = 64
DOCS = 8
COLS = GROUP * ROWS
WIDE = GROUP * DH
NEG = -1e30
RATE = DH ** (-0.5) * 1.4426950408889634

CHIPS = 32
NEAR = 4
FAR = 8


def chip_route(ahead):
    return [(2 * c + k, 2 * ((c + ahead) % CHIPS) + k) for c in range(CHIPS) for k in range(2)]


SIBLING = [(i, i ^ 1) for i in range(2 * CHIPS)]


def bands(docs_ref):
    lane = lax.broadcasted_iota(jnp.int32, (ROWS, DH), 1)
    low = jnp.where(lane == ROWS + DOCS, -(1 << 30), 1 << 30)
    high = jnp.where(lane == ROWS + DOCS, 0, 1 << 30)
    end = jnp.int32(0)
    for d in range(DOCS):
        begin, end = end, end + docs_ref[d]
        low = jnp.where(lane == ROWS + d, begin, low)
        high = jnp.where(lane == ROWS + d, end, high)
    return lane, low, high


def query_marks(here, docs_ref):
    lane, low, high = bands(docs_ref)
    row = lax.broadcasted_iota(jnp.int32, (ROWS, DH), 0)
    pos = here * ROWS + row
    start = jnp.zeros_like(pos)
    end = jnp.int32(0)
    for d in range(DOCS):
        end = end + docs_ref[d]
        start = jnp.where(pos >= end, end, start)
    own = (lane <= row) & (here * ROWS + lane >= start)
    other = ((pos >= low) & (pos < high)) | (lane > ROWS + DOCS)
    marks = jnp.where(lane < ROWS, jnp.where(own, 0.0, NEG), jnp.where(other, 0.0, NEG))
    return marks.astype(jnp.bfloat16)


def key_marks(here, docs_ref, places):
    lane, low, high = bands(docs_ref)
    row = lax.broadcasted_iota(jnp.int32, (ROWS, DH), 0)
    core = lax.rem(here, 2)
    marks = []
    for chips, sibling in places:
        if chips == 0 and not sibling:
            hit = lane == row
        else:
            place = here - 2 * chips
            if sibling:
                place = place + 1 - 2 * core
            if chips == 0:
                place = jnp.where(core == 0, -1, place)
            pos = place * ROWS + row
            hit = (pos >= low) & (pos < high)
        marks.append(jnp.where(hit, 1.0, 0.0).astype(jnp.bfloat16))
    return jnp.concatenate(marks, axis=0)


def flash_kernel(places, first, last, *refs):
    n = len(places)
    here_ref, docs_ref, q_ref = refs[:3]
    kv, refs = refs[3 : 3 + 2 * n], refs[3 + 2 * n :]
    if not first:
        m_in, l_in, acc_in = refs[:3]
        refs = refs[3:]
    if last:
        out_ref, staged, sems = refs
    else:
        m_out, l_out, acc_out = refs

    here = here_ref[0]
    q_marks = jnp.concatenate([query_marks(here, docs_ref)] * GROUP, axis=0)
    k_marks = key_marks(here, docs_ref, places)
    copies = []
    for h in range(HK):
        cols = slice(h * DH, (h + 1) * DH)
        wide = slice(h * WIDE, (h + 1) * WIDE)
        keys = jnp.concatenate([kv[2 * s][:, cols] for s in range(n)], axis=0)
        values = jnp.concatenate([kv[2 * s + 1][:, cols] for s in range(n)], axis=0)
        q = jnp.concatenate([q_ref[:, h * WIDE + g * DH : h * WIDE + (g + 1) * DH] for g in range(GROUP)], axis=0)
        scores = lax.dot_general(
            jnp.concatenate([keys, k_marks], axis=1),
            jnp.concatenate([q, q_marks], axis=1),
            (((1,), (1,)), ((), ())),
            preferred_element_type=jnp.float32,
        )
        top = jnp.max(scores, axis=0, keepdims=True)
        if not first:
            old = m_in[h : h + 1, :]
            top = jnp.maximum(top, old)
        weights = jnp.exp2(scores * RATE - top * RATE)
        total = jnp.sum(weights, axis=0, keepdims=True)
        part = lax.dot_general(
            values, weights.astype(jnp.bfloat16), (((0,), (0,)), ((), ())), preferred_element_type=jnp.float32
        )
        if not first:
            factor = jnp.exp2((old - top) * RATE)
            total = total + l_in[h : h + 1, :] * factor
            part = part + acc_in[h] * factor
        if last:
            result = (part / total).T.astype(jnp.bfloat16)
            for g in range(GROUP):
                staged[:, h * WIDE + g * DH : h * WIDE + (g + 1) * DH] = result[g * ROWS : (g + 1) * ROWS, :]
            copies.append(pltpu.make_async_copy(staged.at[:, wide], out_ref.at[:, wide], sems.at[h]))
            copies[-1].start()
        else:
            m_out[h : h + 1, :] = top
            l_out[h : h + 1, :] = total
            acc_out[h] = part
    for copy in copies:
        copy.wait()


def flash(here, docs, q, shards, places, state, last):
    n = len(places)
    first = state is None
    vmem = pl.BlockSpec(memory_space=pltpu.VMEM)
    smem = pl.BlockSpec(memory_space=pltpu.SMEM)
    operands = [here, docs, q] + list(shards) + ([] if first else list(state))
    if last:
        out_shape = jax.ShapeDtypeStruct((ROWS, HQ * DH), jnp.bfloat16)
        out_specs = pl.BlockSpec(memory_space=pl.ANY)
        scratch = [pltpu.VMEM((ROWS, HQ * DH), jnp.bfloat16), pltpu.SemaphoreType.DMA((HK,))]
    else:
        out_shape = (
            jax.ShapeDtypeStruct((HK, COLS), jnp.float32),
            jax.ShapeDtypeStruct((HK, COLS), jnp.float32),
            jax.ShapeDtypeStruct((HK, DH, COLS), jnp.float32),
        )
        out_specs = (vmem, vmem, vmem)
        scratch = []
    return pl.pallas_call(
        functools.partial(flash_kernel, tuple(places), first, last),
        out_shape=out_shape,
        in_specs=[smem, smem] + [vmem] * (len(operands) - 2),
        out_specs=out_specs,
        scratch_shapes=scratch,
        compiler_params=pltpu.CompilerParams(vmem_limit_bytes=16 * 1024 * 1024),
        cost_estimate=pl.CostEstimate(
            flops=4 * n * ROWS * HQ * ROWS * DH, bytes_accessed=2 << 20, transcendentals=n * ROWS * HQ * ROWS
        ),
    )(*operands)


def per_device(queries, key_heads, value_heads, doc_lengths):
    here = lax.axis_index("seq").astype(jnp.int32).reshape(1)

    def send(block, ahead):
        return lax.ppermute(block, "seq", chip_route(ahead))

    def swap(blocks):
        got = lax.ppermute(jnp.concatenate(blocks, axis=0), "seq", SIBLING)
        return [got[i * ROWS : (i + 1) * ROWS] for i in range(len(blocks))]

    own = (key_heads, value_heads)
    near, far = own, own
    shards = list(own)
    places = [0]
    for step in range(NEAR):
        near = tuple(send(x, 1) for x in near)
        far = tuple(send(x, FAR if step == 0 else -1) for x in far)
        if step < NEAR - 1:
            shards += list(near + far)
            places += [step + 1, FAR - step]
    both = near + far
    both_at = [NEAR, FAR - NEAR + 1]

    def at(chips, sibling):
        return [(c, sibling) for c in chips]

    state = flash(here, doc_lengths, queries, shards, at(places, False), None, False)
    state = flash(here, doc_lengths, queries, swap(shards), at(places, True), state, False)
    both, state = lax.optimization_barrier((both, state))
    return flash(
        here, doc_lengths, queries, list(both) + swap(both), at(both_at, False) + at(both_at, True), state, True
    )


def solution(mesh):
    return jax.shard_map(
        per_device,
        mesh=mesh,
        in_specs=(
            P(("grp", "seq"), None),
            P(("grp", "seq"), None),
            P(("grp", "seq"), None),
            P("grp"),
        ),
        out_specs=P(("grp", "seq"), None),
        check_vma=False,
    )
```

```python
import functools

import jax
import jax.numpy as jnp
from jax import lax
from jax.experimental import pallas as pl
from jax.experimental.pallas import tpu as pltpu
from jax.sharding import PartitionSpec as P

HK = 8
GROUP = 8
DH = 128
HQ = 64
ROWS = 64
DOCS = 8
COLS = GROUP * ROWS
WIDE = GROUP * DH
NEG = -1e30
RATE = DH ** (-0.5) * 1.4426950408889634

CHIPS = 32
NEAR = 4
FAR = 8


def chip_route(ahead):
    return [(2 * c + k, 2 * ((c + ahead) % CHIPS) + k) for c in range(CHIPS) for k in range(2)]


SIBLING = [(i, i ^ 1) for i in range(2 * CHIPS)]


def bands(docs_ref):
    lane = lax.broadcasted_iota(jnp.int32, (ROWS, DH), 1)
    low = jnp.where(lane == ROWS + DOCS, -(1 << 30), 1 << 30)
    high = jnp.where(lane == ROWS + DOCS, 0, 1 << 30)
    end = jnp.int32(0)
    for d in range(DOCS):
        begin, end = end, end + docs_ref[d]
        low = jnp.where(lane == ROWS + d, begin, low)
        high = jnp.where(lane == ROWS + d, end, high)
    return lane, low, high


def query_marks(here, docs_ref):
    lane, low, high = bands(docs_ref)
    row = lax.broadcasted_iota(jnp.int32, (ROWS, DH), 0)
    pos = here * ROWS + row
    start = jnp.zeros_like(pos)
    end = jnp.int32(0)
    for d in range(DOCS):
        end = end + docs_ref[d]
        start = jnp.where(pos >= end, end, start)
    own = (lane <= row) & (here * ROWS + lane >= start)
    other = ((pos >= low) & (pos < high)) | (lane > ROWS + DOCS)
    marks = jnp.where(lane < ROWS, jnp.where(own, 0.0, NEG), jnp.where(other, 0.0, NEG))
    return marks.astype(jnp.bfloat16)


def key_marks(here, docs_ref, places):
    lane, low, high = bands(docs_ref)
    row = lax.broadcasted_iota(jnp.int32, (ROWS, DH), 0)
    core = lax.rem(here, 2)
    marks = []
    for chips, sibling in places:
        if chips == 0 and not sibling:
            hit = lane == row
        else:
            place = here - 2 * chips
            if sibling:
                place = place + 1 - 2 * core
            if chips == 0:
                place = jnp.where(core == 0, -1, place)
            pos = place * ROWS + row
            hit = (pos >= low) & (pos < high)
        marks.append(jnp.where(hit, 1.0, 0.0).astype(jnp.bfloat16))
    return jnp.concatenate(marks, axis=0)


def flash_kernel(blocks, places, first, last, *refs):
    n_kv = 1 + max(max(k[0], v[0]) for k, v in blocks)
    here_ref, docs_ref, q_ref = refs[:3]
    kv, refs = refs[3 : 3 + n_kv], refs[3 + n_kv :]
    if not first:
        m_in, l_in, acc_in = refs[:3]
        refs = refs[3:]
    if last:
        out_ref, staged, sems = refs
    else:
        m_out, l_out, acc_out = refs

    here = here_ref[0]
    q_marks = jnp.concatenate([query_marks(here, docs_ref)] * GROUP, axis=0)
    k_marks = key_marks(here, docs_ref, places)

    def shards(which, h):
        parts = [kv[pair[which][0]][pair[which][1] : pair[which][1] + ROWS, h * DH : (h + 1) * DH] for pair in blocks]
        return jnp.concatenate(parts, axis=0)

    scores = []
    for h in range(HK):
        q = jnp.concatenate([q_ref[:, h * WIDE + g * DH : h * WIDE + (g + 1) * DH] for g in range(GROUP)], axis=0)
        scores.append(
            lax.dot_general(
                jnp.concatenate([shards(0, h), k_marks], axis=1),
                jnp.concatenate([q, q_marks], axis=1),
                (((1,), (1,)), ((), ())),
                preferred_element_type=jnp.float32,
            )
        )
    tops, totals, weights = [], [], []
    for h in range(HK):
        top = jnp.max(scores[h], axis=0, keepdims=True)
        if not first:
            top = jnp.maximum(top, m_in[h : h + 1, :])
        weight = jnp.exp2(scores[h] * RATE - top * RATE)
        tops.append(top)
        totals.append(jnp.sum(weight, axis=0, keepdims=True))
        weights.append(weight.astype(jnp.bfloat16))
    copies = []
    for h in range(HK):
        wide = slice(h * WIDE, (h + 1) * WIDE)
        total = totals[h]
        part = lax.dot_general(
            shards(1, h), weights[h], (((0,), (0,)), ((), ())), preferred_element_type=jnp.float32
        )
        if not first:
            factor = jnp.exp2((m_in[h : h + 1, :] - tops[h]) * RATE)
            total = total + l_in[h : h + 1, :] * factor
            part = part + acc_in[h] * factor
        if last:
            result = (part / total).T.astype(jnp.bfloat16)
            for g in range(GROUP):
                staged[:, h * WIDE + g * DH : h * WIDE + (g + 1) * DH] = result[g * ROWS : (g + 1) * ROWS, :]
            copies.append(pltpu.make_async_copy(staged.at[:, wide], out_ref.at[:, wide], sems.at[h]))
            copies[-1].start()
        else:
            m_out[h : h + 1, :] = tops[h]
            l_out[h : h + 1, :] = total
            acc_out[h] = part
    for copy in copies:
        copy.wait()


VMEM = pl.BlockSpec(memory_space=pltpu.VMEM)
SMEM = pl.BlockSpec(memory_space=pltpu.SMEM)
HBM = pl.BlockSpec(memory_space=pl.ANY)
PARAMS = pltpu.CompilerParams(vmem_limit_bytes=16 * 1024 * 1024)


def flash(here, docs, q, arrays, blocks, places, state, last):
    n = len(places)
    first = state is None
    operands = [here, docs, q] + list(arrays) + ([] if first else list(state))
    if last:
        out_shape = jax.ShapeDtypeStruct((ROWS, HQ * DH), jnp.bfloat16)
        out_specs = HBM
        scratch = [pltpu.VMEM((ROWS, HQ * DH), jnp.bfloat16), pltpu.SemaphoreType.DMA((HK,))]
    else:
        out_shape = (
            jax.ShapeDtypeStruct((HK, COLS), jnp.float32),
            jax.ShapeDtypeStruct((HK, COLS), jnp.float32),
            jax.ShapeDtypeStruct((HK, DH, COLS), jnp.float32),
        )
        out_specs = (VMEM, VMEM, VMEM)
        scratch = []
    return pl.pallas_call(
        functools.partial(flash_kernel, tuple(blocks), tuple(places), first, last),
        out_shape=out_shape,
        in_specs=[SMEM, SMEM] + [VMEM] * (len(operands) - 2),
        out_specs=out_specs,
        scratch_shapes=scratch,
        compiler_params=PARAMS,
        cost_estimate=pl.CostEstimate(
            flops=4 * n * ROWS * HQ * ROWS * DH, bytes_accessed=1 << 16, transcendentals=n * ROWS * HQ * ROWS
        ),
    )(*operands)


def pack_kernel(n, *refs):
    out_ref = refs[-1]
    for i in range(n):
        out_ref[i * ROWS : (i + 1) * ROWS, :] = refs[i][...]


def pack(blocks, after):
    n = len(blocks)
    return pl.pallas_call(
        functools.partial(pack_kernel, n),
        out_shape=jax.ShapeDtypeStruct((n * ROWS, HK * DH), jnp.bfloat16),
        in_specs=[VMEM] * n + [HBM],
        out_specs=VMEM,
        compiler_params=PARAMS,
        cost_estimate=pl.CostEstimate(flops=0, bytes_accessed=1 << 16, transcendentals=0),
    )(*blocks, after)


def apart(n):
    return [((2 * s, 0), (2 * s + 1, 0)) for s in range(n)]


def stacked(n, array=0):
    return [((array, 2 * s * ROWS), (array, (2 * s + 1) * ROWS)) for s in range(n)]


def per_device(queries, key_heads, value_heads, doc_lengths):
    here = lax.axis_index("seq").astype(jnp.int32).reshape(1)

    def send(block, ahead):
        return lax.ppermute(block, "seq", chip_route(ahead))

    def swap(block):
        return lax.ppermute(block, "seq", SIBLING)

    own = (key_heads, value_heads)
    near, far = own, own
    shards = list(own)
    chips = [0]
    for step in range(NEAR):
        near = tuple(send(x, 1) for x in near)
        far = tuple(send(x, FAR if step == 0 else -1) for x in far)
        if step < NEAR - 1:
            shards += list(near + far)
            chips += [step + 1, FAR - step]
    end = near + far
    end_chips = [NEAR, FAR - NEAR + 1]

    def at(chips, sibling):
        return [(c, sibling) for c in chips]

    n = len(chips)
    other = swap(pack(shards, far[0]))
    state = flash(here, doc_lengths, queries, shards, apart(n), at(chips, False), None, False)
    state = flash(here, doc_lengths, queries, [other], stacked(n), at(chips, True), state, False)
    end, state = lax.optimization_barrier((end, state))
    other = swap(jnp.concatenate(end, axis=0))
    return flash(
        here,
        doc_lengths,
        queries,
        list(end) + [other],
        apart(2) + stacked(2, 4),
        at(end_chips, False) + at(end_chips, True),
        state,
        True,
    )


def solution(mesh):
    return jax.shard_map(
        per_device,
        mesh=mesh,
        in_specs=(
            P(("grp", "seq"), None),
            P(("grp", "seq"), None),
            P(("grp", "seq"), None),
            P("grp"),
        ),
        out_specs=P(("grp", "seq"), None),
        check_vma=False,
    )
```

```python
import functools

import jax
import jax.numpy as jnp
from jax import lax
from jax.experimental import pallas as pl
from jax.experimental.pallas import tpu as pltpu
from jax.sharding import PartitionSpec as P

HK = 8
GROUP = 8
DH = 128
HQ = 64
ROWS = 64
DOCS = 8
COLS = GROUP * ROWS
WIDE = GROUP * DH
NEG = -1e30
RATE = DH ** (-0.5) * 1.4426950408889634

CHIPS = 32
NEAR = 4
FAR = 8


def chip_route(ahead):
    return [(2 * c + k, 2 * ((c + ahead) % CHIPS) + k) for c in range(CHIPS) for k in range(2)]


SIBLING = [(i, i ^ 1) for i in range(2 * CHIPS)]


def bands(docs_ref):
    lane = lax.broadcasted_iota(jnp.int32, (ROWS, DH), 1)
    low = jnp.where(lane == ROWS + DOCS, -(1 << 30), 1 << 30)
    high = jnp.where(lane == ROWS + DOCS, 0, 1 << 30)
    end = jnp.int32(0)
    for d in range(DOCS):
        begin, end = end, end + docs_ref[d]
        low = jnp.where(lane == ROWS + d, begin, low)
        high = jnp.where(lane == ROWS + d, end, high)
    return lane, low, high


def query_marks(here, docs_ref):
    lane, low, high = bands(docs_ref)
    row = lax.broadcasted_iota(jnp.int32, (ROWS, DH), 0)
    pos = here * ROWS + row
    start = jnp.zeros_like(pos)
    end = jnp.int32(0)
    for d in range(DOCS):
        end = end + docs_ref[d]
        start = jnp.where(pos >= end, end, start)
    own = (lane <= row) & (here * ROWS + lane >= start)
    other = ((pos >= low) & (pos < high)) | (lane > ROWS + DOCS)
    marks = jnp.where(lane < ROWS, jnp.where(own, 0.0, NEG), jnp.where(other, 0.0, NEG))
    return marks.astype(jnp.bfloat16)


def key_marks(here, docs_ref, places):
    lane, low, high = bands(docs_ref)
    row = lax.broadcasted_iota(jnp.int32, (ROWS, DH), 0)
    core = lax.rem(here, 2)
    marks = []
    for chips, sibling in places:
        if chips == 0 and not sibling:
            hit = lane == row
        else:
            place = here - 2 * chips
            if sibling:
                place = place + 1 - 2 * core
            if chips == 0:
                place = jnp.where(core == 0, -1, place)
            pos = place * ROWS + row
            hit = (pos >= low) & (pos < high)
        marks.append(jnp.where(hit, 1.0, 0.0).astype(jnp.bfloat16))
    return jnp.concatenate(marks, axis=0)


def flash_kernel(n, places, kind, *refs):
    here_ref, docs_ref, q_ref = refs[:3]
    if kind == "end":
        kv, refs = refs[3:8], refs[8:]
        m_in, l_in, acc_in, *lent, out_ref, staged, sems = refs
    else:
        kv, refs = refs[3 : 3 + 2 * n], refs[3 + 2 * n :]

    here = here_ref[0]
    q_marks = jnp.concatenate([query_marks(here, docs_ref)] * GROUP, axis=0)
    k_marks = key_marks(here, docs_ref, places)

    def shards(which, h):
        cols = slice(h * DH, (h + 1) * DH)
        if kind == "end":
            parts = [kv[which][:, cols], kv[2 + which][:, cols]]
            parts += [kv[4][(2 * s + which) * ROWS : (2 * s + which + 1) * ROWS, cols] for s in range(2)]
        else:
            parts = [kv[2 * s + which][:, cols] for s in range(n)]
        return jnp.concatenate(parts, axis=0)

    scores = []
    for h in range(HK):
        q = jnp.concatenate([q_ref[:, h * WIDE + g * DH : h * WIDE + (g + 1) * DH] for g in range(GROUP)], axis=0)
        scores.append(
            lax.dot_general(
                jnp.concatenate([shards(0, h), k_marks], axis=1),
                jnp.concatenate([q, q_marks], axis=1),
                (((1,), (1,)), ((), ())),
                preferred_element_type=jnp.float32,
            )
        )
    if kind == "end":
        m_lent, l_lent = lent_stats(lent)
        known = jnp.maximum(m_in[...], m_lent)
    tops, totals, weights = [], [], []
    for h in range(HK):
        top = jnp.max(scores[h], axis=0, keepdims=True)
        if kind == "end":
            top = jnp.maximum(top, known[h : h + 1, :])
        weight = jnp.exp2(scores[h] * RATE - top * RATE)
        tops.append(top)
        totals.append(jnp.sum(weight, axis=0, keepdims=True))
        weights.append(weight.astype(jnp.bfloat16))
    if kind == "lend":
        lent = refs
        for i in range(HALVES):
            half = slice(i * HALF, (i + 1) * HALF)
            pieces = in_three(jnp.concatenate(tops[half], axis=0)) + in_three(jnp.concatenate(totals[half], axis=0))
            pieces += [jnp.zeros((STATS - 6 * HALF, COLS), jnp.float32)]
            lent[i][HALF * DH :, :] = jnp.concatenate(pieces, axis=0).astype(jnp.bfloat16)
    if kind == "own":
        m_out, l_out, acc_out = refs
        m_out[...] = jnp.concatenate(tops, axis=0)
        l_out[...] = jnp.concatenate(totals, axis=0)
    copies = []
    for h in range(HK):
        part = lax.dot_general(
            shards(1, h), weights[h], (((0,), (0,)), ((), ())), preferred_element_type=jnp.float32
        )
        if kind == "own":
            acc_out[h] = part
        if kind == "lend":
            lent[h // HALF][h % HALF * DH : (h % HALF + 1) * DH, :] = (part * (1.0 / totals[h])).astype(jnp.bfloat16)
        if kind == "end":
            wide = slice(h * WIDE, (h + 1) * WIDE)
            held = jnp.exp2((m_in[h : h + 1, :] - tops[h]) * RATE)
            got = l_lent[h : h + 1, :] * jnp.exp2((m_lent[h : h + 1, :] - tops[h]) * RATE)
            share = 1.0 / (totals[h] + l_in[h : h + 1, :] * held + got)
            part = part * share + acc_in[h] * (held * share)
            part = part + lent[h // HALF][h % HALF * DH : (h % HALF + 1) * DH, :].astype(jnp.float32) * (got * share)
            result = part.T.astype(jnp.bfloat16)
            for g in range(GROUP):
                staged[:, h * WIDE + g * DH : h * WIDE + (g + 1) * DH] = result[g * ROWS : (g + 1) * ROWS, :]
            copies.append(pltpu.make_async_copy(staged.at[:, wide], out_ref.at[:, wide], sems.at[h]))
            copies[-1].start()
    for copy in copies:
        copy.wait()


HALVES = 2
HALF = HK // HALVES
STATS = 32


def in_three(x):
    pieces = []
    for _ in range(3):
        pieces.append(x.astype(jnp.bfloat16).astype(jnp.float32))
        x = x - pieces[-1]
    return pieces


def lent_stats(lent):
    tops, totals = [], []
    for half in lent:
        stats = half[HALF * DH :, :].astype(jnp.float32)
        pieces = [stats[i * HALF : (i + 1) * HALF, :] for i in range(6)]
        tops.append(pieces[0] + pieces[1] + pieces[2])
        totals.append(pieces[3] + pieces[4] + pieces[5])
    return jnp.concatenate(tops, axis=0), jnp.concatenate(totals, axis=0)


VMEM = pl.BlockSpec(memory_space=pltpu.VMEM)
SMEM = pl.BlockSpec(memory_space=pltpu.SMEM)
HBM = pl.BlockSpec(memory_space=pl.ANY)


def flash(kind, here, docs, q, arrays, places):
    n = len(places)
    operands = [here, docs, q] + list(arrays)
    scratch = []
    out_specs = VMEM
    if kind == "end":
        out_shape = jax.ShapeDtypeStruct((ROWS, HQ * DH), jnp.bfloat16)
        out_specs = HBM
        scratch = [pltpu.VMEM((ROWS, HQ * DH), jnp.bfloat16), pltpu.SemaphoreType.DMA((HK,))]
    elif kind == "lend":
        out_specs = (VMEM,) * HALVES
        out_shape = (jax.ShapeDtypeStruct((HALF * DH + STATS, COLS), jnp.bfloat16),) * HALVES
    else:
        out_specs = (VMEM, VMEM, VMEM)
        out_shape = (
            jax.ShapeDtypeStruct((HK, COLS), jnp.float32),
            jax.ShapeDtypeStruct((HK, COLS), jnp.float32),
            jax.ShapeDtypeStruct((HK, DH, COLS), jnp.float32),
        )
    return pl.pallas_call(
        functools.partial(flash_kernel, n, tuple(places), kind),
        out_shape=out_shape,
        in_specs=[SMEM, SMEM] + [VMEM] * (len(operands) - 2),
        out_specs=out_specs,
        scratch_shapes=scratch,
        compiler_params=pltpu.CompilerParams(vmem_limit_bytes=16 * 1024 * 1024),
        cost_estimate=pl.CostEstimate(
            flops=4 * n * ROWS * HQ * ROWS * DH, bytes_accessed=1 << 16, transcendentals=n * ROWS * HQ * ROWS
        ),
    )(*operands)


def per_device(queries, key_heads, value_heads, doc_lengths):
    here = lax.axis_index("seq").astype(jnp.int32).reshape(1)
    there = here + 1 - 2 * lax.rem(here, 2)

    def send(block, ahead):
        return lax.ppermute(block, "seq", chip_route(ahead))

    def swap(block):
        return lax.ppermute(block, "seq", SIBLING)

    own = (key_heads, value_heads)
    near, far = own, own
    shards = list(own)
    chips = [0]
    for step in range(NEAR):
        near = tuple(send(x, 1) for x in near)
        far = tuple(send(x, FAR if step == 0 else -1) for x in far)
        if step < NEAR - 1:
            shards += list(near + far)
            chips += [step + 1, FAR - step]
    end = near + far
    end_chips = [NEAR, FAR - NEAR + 1]

    lent = flash("lend", there, doc_lengths, swap(queries), shards, [(c, True) for c in chips])
    got = [swap(x) for x in lent]
    state = flash("own", here, doc_lengths, queries, shards, [(c, False) for c in chips])
    end, state, _ = lax.optimization_barrier((end, state, lent))
    arrays = list(end) + [swap(jnp.concatenate(end, axis=0))] + list(state) + got
    places = [(c, False) for c in end_chips] + [(c, True) for c in end_chips]
    return flash("end", here, doc_lengths, queries, arrays, places)


def solution(mesh):
    return jax.shard_map(
        per_device,
        mesh=mesh,
        in_specs=(
            P(("grp", "seq"), None),
            P(("grp", "seq"), None),
            P(("grp", "seq"), None),
            P("grp"),
        ),
        out_specs=P(("grp", "seq"), None),
        check_vma=False,
    )
```

```python
import functools

import jax
import jax.numpy as jnp
from jax import lax
from jax.experimental import pallas as pl
from jax.experimental.pallas import tpu as pltpu
from jax.sharding import PartitionSpec as P

HK = 8
GROUP = 8
DH = 128
HQ = 64
ROWS = 64
DOCS = 8
COLS = GROUP * ROWS
WIDE = GROUP * DH
NEG = -1e30
RATE = DH ** (-0.5) * 1.4426950408889634

CHIPS = 32
NEAR = 4
FAR = 8


def chip_route(ahead):
    return [(2 * c + k, 2 * ((c + ahead) % CHIPS) + k) for c in range(CHIPS) for k in range(2)]


SIBLING = [(i, i ^ 1) for i in range(2 * CHIPS)]


def bands(info_ref):
    lane = lax.broadcasted_iota(jnp.int32, (ROWS, DH), 1)
    low = jnp.where(lane == ROWS + DOCS, -(1 << 30), 1 << 30)
    high = jnp.where(lane == ROWS + DOCS, 0, 1 << 30)
    end = jnp.int32(0)
    for d in range(DOCS):
        begin, end = end, end + info_ref[1 + d]
        low = jnp.where(lane == ROWS + d, begin, low)
        high = jnp.where(lane == ROWS + d, end, high)
    return lane, low, high


def query_marks(here, info_ref):
    lane, low, high = bands(info_ref)
    row = lax.broadcasted_iota(jnp.int32, (ROWS, DH), 0)
    pos = here * ROWS + row
    start = jnp.zeros_like(pos)
    end = jnp.int32(0)
    for d in range(DOCS):
        end = end + info_ref[1 + d]
        start = jnp.where(pos >= end, end, start)
    own = (lane <= row) & (here * ROWS + lane >= start)
    other = ((pos >= low) & (pos < high)) | (lane > ROWS + DOCS)
    marks = jnp.where(lane < ROWS, jnp.where(own, 0.0, NEG), jnp.where(other, 0.0, NEG))
    return marks.astype(jnp.bfloat16)


def key_marks(here, info_ref, places):
    lane, low, high = bands(info_ref)
    row = lax.broadcasted_iota(jnp.int32, (ROWS, DH), 0)
    core = lax.rem(here, 2)
    marks = []
    for chips, sibling in places:
        if chips == 0 and not sibling:
            hit = lane == row
        else:
            place = here - 2 * chips
            if sibling:
                place = place + 1 - 2 * core
            if chips == 0:
                place = jnp.where(core == 0, -1, place)
            pos = place * ROWS + row
            hit = (pos >= low) & (pos < high)
        marks.append(jnp.where(hit, 1.0, 0.0).astype(jnp.bfloat16))
    return jnp.concatenate(marks, axis=0)


def flash_kernel(n, places, kind, *refs):
    info_ref, q_ref = refs[:2]
    if kind == "end":
        kv, refs = refs[2:7], refs[7:]
        m_in, l_in, acc_in, *lent, out_ref, staged, sems = refs
    else:
        kv, refs = refs[2 : 1 + 2 * n], refs[1 + 2 * n :]

    here = info_ref[0]
    if kind == "lend":
        lent = refs
    q_marks = jnp.concatenate([query_marks(here, info_ref)] * GROUP, axis=0)
    k_marks = key_marks(here, info_ref, places)

    def shards(which, h):
        cols = slice(h * DH, (h + 1) * DH)
        if kind == "end":
            parts = [kv[which][:, cols], kv[2 + which][:, cols]]
            parts += [kv[4][(2 * s + which) * ROWS : (2 * s + which + 1) * ROWS, cols] for s in range(2)]
        else:
            parts = [kv[0][which * ROWS : (which + 1) * ROWS, cols]]
            parts += [kv[2 * s - 1 + which][:, cols] for s in range(1, n)]
        return jnp.concatenate(parts, axis=0)

    scores = []
    for h in range(HK):
        q = jnp.concatenate([q_ref[:, h * WIDE + g * DH : h * WIDE + (g + 1) * DH] for g in range(GROUP)], axis=0)
        scores.append(
            lax.dot_general(
                jnp.concatenate([shards(0, h), k_marks], axis=1),
                jnp.concatenate([q, q_marks], axis=1),
                (((1,), (1,)), ((), ())),
                preferred_element_type=jnp.float32,
            )
        )
    if kind == "end":
        m_lent, l_lent = lent_stats(lent)
        known = jnp.maximum(m_in[...], m_lent)
    tops, totals, weights = [], [], []
    for h in range(HK):
        top = jnp.max(scores[h], axis=0, keepdims=True)
        if kind == "end":
            top = jnp.maximum(top, known[h : h + 1, :])
        weight = jnp.exp2(scores[h] * RATE - top * RATE)
        tops.append(top)
        totals.append(jnp.sum(weight, axis=0, keepdims=True))
        weights.append(weight.astype(jnp.bfloat16))
    if kind == "lend":
        for i, (low, high) in enumerate(LOTS):
            pieces = in_three(jnp.concatenate(tops[low:high], axis=0)) + in_three(
                jnp.concatenate(totals[low:high], axis=0)
            )
            if STATS > 6 * (high - low):
                pieces += [jnp.zeros((STATS - 6 * (high - low), COLS), jnp.float32)]
            lent[i][(high - low) * DH : (high - low) * DH + STATS, :] = jnp.concatenate(pieces, axis=0).astype(jnp.bfloat16)
    if kind == "own":
        m_out, l_out, acc_out = refs
        m_out[...] = jnp.concatenate(tops, axis=0)
        l_out[...] = jnp.concatenate(totals, axis=0)
    copies = []
    for h in range(HK):
        part = lax.dot_general(
            shards(1, h), weights[h], (((0,), (0,)), ((), ())), preferred_element_type=jnp.float32
        )
        if kind == "own":
            acc_out[h] = part
        if kind == "lend":
            i, j = lot_of(h)
            lent[i][j * DH : (j + 1) * DH, :] = (part * (1.0 / totals[h])).astype(jnp.bfloat16)
        if kind == "end":
            wide = slice(h * WIDE, (h + 1) * WIDE)
            held = jnp.exp2((m_in[h : h + 1, :] - tops[h]) * RATE)
            got = l_lent[h : h + 1, :] * jnp.exp2((m_lent[h : h + 1, :] - tops[h]) * RATE)
            share = 1.0 / (totals[h] + l_in[h : h + 1, :] * held + got)
            part = part * share + acc_in[h] * (held * share)
            i, j = lot_of(h)
            part = part + lent[i][j * DH : (j + 1) * DH, :].astype(jnp.float32) * (got * share)
            result = part.T.astype(jnp.bfloat16)
            for g in range(GROUP):
                staged[:, h * WIDE + g * DH : h * WIDE + (g + 1) * DH] = result[g * ROWS : (g + 1) * ROWS, :]
            copies.append(pltpu.make_async_copy(staged.at[:, wide], out_ref.at[:, wide], sems.at[h]))
            copies[-1].start()
    for copy in copies:
        copy.wait()


LOTS = ((0, 4), (4, 8))
STATS = 32
LENT = 640


def lot_of(h):
    for i, (low, high) in enumerate(LOTS):
        if low <= h < high:
            return i, h - low


def in_three(x):
    pieces = []
    for _ in range(3):
        pieces.append(x.astype(jnp.bfloat16).astype(jnp.float32))
        x = x - pieces[-1]
    return pieces


def lent_stats(lent):
    tops, totals = [], []
    for lot, (low, high) in zip(lent, LOTS):
        n = high - low
        stats = lot[n * DH : n * DH + STATS, :].astype(jnp.float32)
        pieces = [stats[i * n : (i + 1) * n, :] for i in range(6)]
        tops.append(pieces[0] + pieces[1] + pieces[2])
        totals.append(pieces[3] + pieces[4] + pieces[5])
    return jnp.concatenate(tops, axis=0), jnp.concatenate(totals, axis=0)


VMEM = pl.BlockSpec(memory_space=pltpu.VMEM)
SMEM = pl.BlockSpec(memory_space=pltpu.SMEM)
HBM = pl.BlockSpec(memory_space=pl.ANY)


def flash(kind, info, q, arrays, places):
    n = len(places)
    operands = [info, q] + list(arrays)
    in_specs = [SMEM] + [VMEM] * (len(operands) - 1)
    scratch = []
    out_specs = VMEM
    if kind == "end":
        out_shape = jax.ShapeDtypeStruct((ROWS, HQ * DH), jnp.bfloat16)
        out_specs = HBM
        scratch = [pltpu.VMEM((ROWS, HQ * DH), jnp.bfloat16), pltpu.SemaphoreType.DMA((HK,))]
    elif kind == "lend":
        out_specs = (VMEM,) * len(LOTS)
        out_shape = tuple(
            jax.ShapeDtypeStruct((LENT, COLS), jnp.bfloat16) for low, high in LOTS
        )
    else:
        out_specs = (VMEM, VMEM, VMEM)
        out_shape = (
            jax.ShapeDtypeStruct((HK, COLS), jnp.float32),
            jax.ShapeDtypeStruct((HK, COLS), jnp.float32),
            jax.ShapeDtypeStruct((HK, DH, COLS), jnp.float32),
        )
    return pl.pallas_call(
        functools.partial(flash_kernel, n, tuple(places), kind),
        out_shape=out_shape,
        in_specs=in_specs,
        out_specs=out_specs,
        scratch_shapes=scratch,
        compiler_params=pltpu.CompilerParams(vmem_limit_bytes=16 * 1024 * 1024),
        cost_estimate=pl.CostEstimate(
            flops=4 * n * ROWS * HQ * ROWS * DH, bytes_accessed=1 << 16, transcendentals=n * ROWS * HQ * ROWS
        ),
    )(*operands)


def per_device(queries, key_heads, value_heads, doc_lengths):
    here = lax.axis_index("seq").astype(jnp.int32).reshape(1)
    there = here + 1 - 2 * lax.rem(here, 2)
    info, info_there = (jnp.concatenate([place, doc_lengths]) for place in (here, there))

    def send(block, ahead):
        return lax.ppermute(block, "seq", chip_route(ahead))

    def swap(block):
        return lax.ppermute(block, "seq", SIBLING)

    own = (key_heads, value_heads)
    near, far = own, own
    shards = [jnp.concatenate(own, axis=0)]
    chips = [0]
    for step in range(NEAR):
        near = tuple(send(x, 1) for x in near)
        far = tuple(send(x, FAR if step == 0 else -1) for x in far)
        if step == 0:
            first, shards[0] = lax.optimization_barrier((far[0], shards[0]))
            far = (first, far[1])
        if step < NEAR - 1:
            shards += list(near + far)
            chips += [step + 1, FAR - step]
    end = near + far
    end_chips = [NEAR, FAR - NEAR + 1]

    lent = flash("lend", info_there, swap(queries), shards, [(c, True) for c in chips])
    got = [swap(x) for x in lent]
    q, _ = lax.optimization_barrier((queries, lent))
    state = flash("own", info, q, shards, [(c, False) for c in chips])
    end, state = lax.optimization_barrier((end, state))
    arrays = list(end) + [swap(jnp.concatenate(end, axis=0))] + list(state) + got
    places = [(c, False) for c in end_chips] + [(c, True) for c in end_chips]
    return flash("end", info, queries, arrays, places)


def solution(mesh):
    return jax.shard_map(
        per_device,
        mesh=mesh,
        in_specs=(
            P(("grp", "seq"), None),
            P(("grp", "seq"), None),
            P(("grp", "seq"), None),
            P("grp"),
        ),
        out_specs=P(("grp", "seq"), None),
        check_vma=False,
    )
```

```python
import functools

import jax
import jax.numpy as jnp
from jax import lax
from jax.experimental import pallas as pl
from jax.experimental.pallas import tpu as pltpu
from jax.sharding import PartitionSpec as P

HK = 8
GROUP = 8
DH = 128
HQ = 64
ROWS = 64
DOCS = 8
COLS = GROUP * ROWS
WIDE = GROUP * DH
NEG = -1e30
RATE = DH ** (-0.5) * 1.4426950408889634

CHIPS = 32
NEAR = 4
FAR = 8


def chip_route(ahead):
    return [(2 * c + k, 2 * ((c + ahead) % CHIPS) + k) for c in range(CHIPS) for k in range(2)]


SIBLING = [(i, i ^ 1) for i in range(2 * CHIPS)]


def bands(info_ref):
    lane = lax.broadcasted_iota(jnp.int32, (ROWS, DH), 1)
    low = jnp.where(lane == ROWS + DOCS, -(1 << 30), 1 << 30)
    high = jnp.where(lane == ROWS + DOCS, 0, 1 << 30)
    end = jnp.int32(0)
    for d in range(DOCS):
        begin, end = end, end + info_ref[1 + d]
        low = jnp.where(lane == ROWS + d, begin, low)
        high = jnp.where(lane == ROWS + d, end, high)
    return lane, low, high


def query_marks(here, info_ref):
    lane, low, high = bands(info_ref)
    row = lax.broadcasted_iota(jnp.int32, (ROWS, DH), 0)
    pos = here * ROWS + row
    start = jnp.zeros_like(pos)
    end = jnp.int32(0)
    for d in range(DOCS):
        end = end + info_ref[1 + d]
        start = jnp.where(pos >= end, end, start)
    own = (lane <= row) & (here * ROWS + lane >= start)
    other = ((pos >= low) & (pos < high)) | (lane > ROWS + DOCS)
    marks = jnp.where(lane < ROWS, jnp.where(own, 0.0, NEG), jnp.where(other, 0.0, NEG))
    return marks.astype(jnp.bfloat16)


def key_marks(here, info_ref, places):
    lane, low, high = bands(info_ref)
    row = lax.broadcasted_iota(jnp.int32, (ROWS, DH), 0)
    core = lax.rem(here, 2)
    marks = []
    for chips, sibling in places:
        if chips == 0 and not sibling:
            hit = lane == row
        else:
            place = here - 2 * chips
            if sibling:
                place = place + 1 - 2 * core
            if chips == 0:
                place = jnp.where(core == 0, -1, place)
            pos = place * ROWS + row
            hit = (pos >= low) & (pos < high)
        marks.append(jnp.where(hit, 1.0, 0.0).astype(jnp.bfloat16))
    return jnp.concatenate(marks, axis=0)


def flash_kernel(places, kind, *refs):
    n = len(places)
    info_ref, q_ref = refs[:2]
    n_kv = 5 if kind == "end" else 2 * n - 1
    kv, refs = refs[2 : 2 + n_kv], refs[2 + n_kv :]

    here = info_ref[0]
    start = jnp.int32(0)
    end = jnp.int32(0)
    for d in range(DOCS):
        end = end + info_ref[1 + d]
        start = jnp.where(here * ROWS >= end, end, start)

    def reach(some):
        nearest = here - 2 * min(places[s][0] for s in some) + 1
        return nearest * ROWS + ROWS - 1 >= start

    base = [s for s in range(n) if places[s][0] == 0]
    near = [s for s in range(n) if 0 < places[s][0] <= NEAR]
    far = [s for s in range(n) if places[s][0] > NEAR]
    all_reach, near_reach = reach(far), reach(near)

    def attend(some):
        attend_some(some, places, kind, info_ref, q_ref, kv, refs)

    pl.when(all_reach)(lambda: attend(base + near + far))
    pl.when(near_reach & jnp.logical_not(all_reach))(lambda: attend(base + near))
    pl.when(jnp.logical_not(near_reach))(lambda: attend(base))


def attend_some(some, places, kind, info_ref, q_ref, kv, refs):
    here = info_ref[0]
    if kind == "lend":
        lent = refs
    if kind == "end":
        m_in, l_in, acc_in, *lent, out_ref, staged, sems = refs

    def shards(which, h):
        cols = slice(h * DH, (h + 1) * DH)
        parts = []
        for s in some:
            if kind == "end" and s >= 2:
                parts.append(kv[4][(2 * (s - 2) + which) * ROWS : (2 * (s - 2) + which + 1) * ROWS, cols])
            elif kind == "end":
                parts.append(kv[2 * s + which][:, cols])
            elif s == 0:
                parts.append(kv[0][which * ROWS : (which + 1) * ROWS, cols])
            else:
                parts.append(kv[2 * s - 1 + which][:, cols])
        return jnp.concatenate(parts, axis=0)

    scores = []
    if some:
        q_marks = jnp.concatenate([query_marks(here, info_ref)] * GROUP, axis=0)
        k_marks = key_marks(here, info_ref, [places[s] for s in some])
        for h in range(HK):
            q = jnp.concatenate([q_ref[:, h * WIDE + g * DH : h * WIDE + (g + 1) * DH] for g in range(GROUP)], axis=0)
            scores.append(
                lax.dot_general(
                    jnp.concatenate([shards(0, h), k_marks], axis=1),
                    jnp.concatenate([q, q_marks], axis=1),
                    (((1,), (1,)), ((), ())),
                    preferred_element_type=jnp.float32,
                )
            )
    if kind == "end":
        m_lent, l_lent = lent_stats(lent)
        known = jnp.maximum(m_in[...], m_lent)
    tops, totals, weights = [], [], []
    for h in range(HK):
        if not some:
            tops.append(known[h : h + 1, :])
            continue
        top = jnp.max(scores[h], axis=0, keepdims=True)
        if kind == "end":
            top = jnp.maximum(top, known[h : h + 1, :])
        weight = jnp.exp2(scores[h] * RATE - top * RATE)
        tops.append(top)
        totals.append(jnp.sum(weight, axis=0, keepdims=True))
        weights.append(weight.astype(jnp.bfloat16))
    if kind == "lend":
        for i, (low, high) in enumerate(LOTS):
            pieces = in_three(jnp.concatenate(tops[low:high], axis=0)) + in_three(
                jnp.concatenate(totals[low:high], axis=0)
            )
            if STATS > 6 * (high - low):
                pieces += [jnp.zeros((STATS - 6 * (high - low), COLS), jnp.float32)]
            stats = jnp.concatenate(pieces, axis=0).astype(jnp.bfloat16)
            lent[i][(high - low) * DH : (high - low) * DH + STATS, :] = stats
    if kind == "own":
        m_out, l_out, acc_out = refs
        m_out[...] = jnp.concatenate(tops, axis=0)
        l_out[...] = jnp.concatenate(totals, axis=0)
    copies = []
    for h in range(HK):
        if some:
            part = lax.dot_general(
                shards(1, h), weights[h], (((0,), (0,)), ((), ())), preferred_element_type=jnp.float32
            )
        if kind == "own":
            acc_out[h] = part
        if kind == "lend":
            i, j = lot_of(h)
            lent[i][j * DH : (j + 1) * DH, :] = (part * (1.0 / totals[h])).astype(jnp.bfloat16)
        if kind == "end":
            i, j = lot_of(h)
            wide = slice(h * WIDE, (h + 1) * WIDE)
            held = jnp.exp2((m_in[h : h + 1, :] - tops[h]) * RATE)
            got = l_lent[h : h + 1, :] * jnp.exp2((m_lent[h : h + 1, :] - tops[h]) * RATE)
            total = l_in[h : h + 1, :] * held + got
            if some:
                total = total + totals[h]
            share = 1.0 / total
            result = acc_in[h] * (held * share)
            result = result + lent[i][j * DH : (j + 1) * DH, :].astype(jnp.float32) * (got * share)
            if some:
                result = result + part * share
            result = result.T.astype(jnp.bfloat16)
            for g in range(GROUP):
                staged[:, h * WIDE + g * DH : h * WIDE + (g + 1) * DH] = result[g * ROWS : (g + 1) * ROWS, :]
            copies.append(pltpu.make_async_copy(staged.at[:, wide], out_ref.at[:, wide], sems.at[h]))
            copies[-1].start()
    for copy in copies:
        copy.wait()


LOTS = ((0, 4), (4, 8))
STATS = 32
LENT = 640


def lot_of(h):
    for i, (low, high) in enumerate(LOTS):
        if low <= h < high:
            return i, h - low


def in_three(x):
    pieces = []
    for _ in range(3):
        pieces.append(x.astype(jnp.bfloat16).astype(jnp.float32))
        x = x - pieces[-1]
    return pieces


def lent_stats(lent):
    tops, totals = [], []
    for lot, (low, high) in zip(lent, LOTS):
        n = high - low
        stats = lot[n * DH : n * DH + STATS, :].astype(jnp.float32)
        pieces = [stats[i * n : (i + 1) * n, :] for i in range(6)]
        tops.append(pieces[0] + pieces[1] + pieces[2])
        totals.append(pieces[3] + pieces[4] + pieces[5])
    return jnp.concatenate(tops, axis=0), jnp.concatenate(totals, axis=0)


VMEM = pl.BlockSpec(memory_space=pltpu.VMEM)
SMEM = pl.BlockSpec(memory_space=pltpu.SMEM)
HBM = pl.BlockSpec(memory_space=pl.ANY)


def flash(kind, info, q, arrays, places):
    n = len(places)
    operands = [info, q] + list(arrays)
    in_specs = [SMEM] + [VMEM] * (len(operands) - 1)
    scratch = []
    out_specs = VMEM
    if kind == "end":
        out_shape = jax.ShapeDtypeStruct((ROWS, HQ * DH), jnp.bfloat16)
        out_specs = HBM
        scratch = [pltpu.VMEM((ROWS, HQ * DH), jnp.bfloat16), pltpu.SemaphoreType.DMA((HK,))]
    elif kind == "lend":
        out_specs = (VMEM,) * len(LOTS)
        out_shape = (jax.ShapeDtypeStruct((LENT, COLS), jnp.bfloat16),) * len(LOTS)
    else:
        out_specs = (VMEM, VMEM, VMEM)
        out_shape = (
            jax.ShapeDtypeStruct((HK, COLS), jnp.float32),
            jax.ShapeDtypeStruct((HK, COLS), jnp.float32),
            jax.ShapeDtypeStruct((HK, DH, COLS), jnp.float32),
        )
    return pl.pallas_call(
        functools.partial(flash_kernel, tuple(places), kind),
        out_shape=out_shape,
        in_specs=in_specs,
        out_specs=out_specs,
        scratch_shapes=scratch,
        compiler_params=pltpu.CompilerParams(vmem_limit_bytes=16 * 1024 * 1024),
        cost_estimate=pl.CostEstimate(
            flops=4 * n * ROWS * HQ * ROWS * DH, bytes_accessed=1 << 16, transcendentals=n * ROWS * HQ * ROWS
        ),
    )(*operands)


def per_device(queries, key_heads, value_heads, doc_lengths):
    here = lax.axis_index("seq").astype(jnp.int32).reshape(1)
    there = here + 1 - 2 * lax.rem(here, 2)
    info, info_there = (jnp.concatenate([place, doc_lengths]) for place in (here, there))

    def send(block, ahead):
        return lax.ppermute(block, "seq", chip_route(ahead))

    def swap(block):
        return lax.ppermute(block, "seq", SIBLING)

    own = (key_heads, value_heads)
    near, far = own, own
    shards = [jnp.concatenate(own, axis=0)]
    chips = [0]
    for step in range(NEAR):
        near = tuple(send(x, 1) for x in near)
        far = tuple(send(x, FAR if step == 0 else -1) for x in far)
        if step == 0:
            first, shards[0], info, info_there = lax.optimization_barrier((far[0], shards[0], info, info_there))
            far = (first, far[1])
        if step < NEAR - 1:
            shards += list(near + far)
            chips += [step + 1, FAR - step]
    end = near + far
    end_chips = [NEAR, FAR - NEAR + 1]

    lent = flash("lend", info_there, swap(queries), shards, [(c, True) for c in chips])
    got = [swap(x) for x in lent]
    q, _ = lax.optimization_barrier((queries, lent))
    state = flash("own", info, q, shards, [(c, False) for c in chips])
    end, state = lax.optimization_barrier((end, state))
    arrays = list(end) + [swap(jnp.concatenate(end, axis=0))] + list(state) + got
    places = [(c, False) for c in end_chips] + [(c, True) for c in end_chips]
    return flash("end", info, queries, arrays, places)


def solution(mesh):
    return jax.shard_map(
        per_device,
        mesh=mesh,
        in_specs=(
            P(("grp", "seq"), None),
            P(("grp", "seq"), None),
            P(("grp", "seq"), None),
            P("grp"),
        ),
        out_specs=P(("grp", "seq"), None),
        check_vma=False,
    )
```

```python
import functools

import jax
import jax.numpy as jnp
from jax import lax
from jax.experimental import pallas as pl
from jax.experimental.pallas import tpu as pltpu
from jax.sharding import PartitionSpec as P

HK = 8
GROUP = 8
DH = 128
HQ = 64
ROWS = 64
DOCS = 8
COLS = GROUP * ROWS
WIDE = GROUP * DH
NEG = -1e30
RATE = DH ** (-0.5) * 1.4426950408889634

CHIPS = 32
NEAR = 4
HOPS = ((2, 0), (7, 0), (1, 0), (8, 0), (6, 7), (4, 2), (5, 7), (3, 2))
EARLY = (0, 1, 2, 8, 7, 6)
LATE = (4, 5, 3)


def chip_route(ahead):
    return [(2 * c + k, 2 * ((c + ahead) % CHIPS) + k) for c in range(CHIPS) for k in range(2)]


SIBLING = [(i, i ^ 1) for i in range(2 * CHIPS)]


def bands(info_ref):
    lane = lax.broadcasted_iota(jnp.int32, (ROWS, DH), 1)
    low = jnp.where(lane == ROWS + DOCS, -(1 << 30), 1 << 30)
    high = jnp.where(lane == ROWS + DOCS, 0, 1 << 30)
    end = jnp.int32(0)
    for d in range(DOCS):
        begin, end = end, end + info_ref[1 + d]
        low = jnp.where(lane == ROWS + d, begin, low)
        high = jnp.where(lane == ROWS + d, end, high)
    return lane, low, high


def query_marks(here, info_ref):
    lane, low, high = bands(info_ref)
    row = lax.broadcasted_iota(jnp.int32, (ROWS, DH), 0)
    pos = here * ROWS + row
    start = jnp.zeros_like(pos)
    end = jnp.int32(0)
    for d in range(DOCS):
        end = end + info_ref[1 + d]
        start = jnp.where(pos >= end, end, start)
    own = (lane <= row) & (here * ROWS + lane >= start)
    other = ((pos >= low) & (pos < high)) | (lane > ROWS + DOCS)
    marks = jnp.where(lane < ROWS, jnp.where(own, 0.0, NEG), jnp.where(other, 0.0, NEG))
    return marks.astype(jnp.bfloat16)


def key_marks(here, info_ref, places):
    lane, low, high = bands(info_ref)
    row = lax.broadcasted_iota(jnp.int32, (ROWS, DH), 0)
    core = lax.rem(here, 2)
    marks = []
    for chips, sibling in places:
        if chips == 0 and not sibling:
            hit = lane == row
        else:
            place = here - 2 * chips
            if sibling:
                place = place + 1 - 2 * core
            if chips == 0:
                place = jnp.where(core == 0, -1, place)
            pos = place * ROWS + row
            hit = (pos >= low) & (pos < high)
        marks.append(jnp.where(hit, 1.0, 0.0).astype(jnp.bfloat16))
    return jnp.concatenate(marks, axis=0)


def flash_kernel(blocks, places, kind, *refs):
    n = len(places)
    info_ref, q_ref = refs[:2]
    n_kv = 1 + max(array for array, _ in blocks)
    kv, refs = refs[2 : 2 + n_kv], refs[2 + n_kv :]

    here = info_ref[0]
    start = jnp.int32(0)
    end = jnp.int32(0)
    for d in range(DOCS):
        end = end + info_ref[1 + d]
        start = jnp.where(here * ROWS >= end, end, start)

    def reach(some):
        nearest = here - 2 * min(places[s][0] for s in some) + 1
        return nearest * ROWS + ROWS - 1 >= start

    base = [s for s in range(n) if places[s][0] == 0]
    near = [s for s in range(n) if 0 < places[s][0] <= NEAR]
    far = [s for s in range(n) if places[s][0] > NEAR]
    all_reach, near_reach = reach(far), reach(near)

    def attend(some):
        attend_some(some, blocks, places, kind, info_ref, q_ref, kv, refs)

    pl.when(all_reach)(lambda: attend(base + near + far))
    pl.when(near_reach & jnp.logical_not(all_reach))(lambda: attend(base + near))
    pl.when(jnp.logical_not(near_reach))(lambda: attend(base))


def attend_some(some, blocks, places, kind, info_ref, q_ref, kv, refs):
    here = info_ref[0]
    if kind == "lend":
        lent = refs
    if kind == "end":
        m_in, l_in, acc_in, *lent, out_ref, staged, sems = refs

    def shards(which, h):
        cols = slice(h * DH, (h + 1) * DH)
        parts = []
        for s in some:
            array, row = blocks[s]
            parts.append(kv[array][row + which * ROWS : row + (which + 1) * ROWS, cols])
        return jnp.concatenate(parts, axis=0)

    scores = []
    if some:
        q_marks = jnp.concatenate([query_marks(here, info_ref)] * GROUP, axis=0)
        k_marks = key_marks(here, info_ref, [places[s] for s in some])
        for h in range(HK):
            q = jnp.concatenate([q_ref[:, h * WIDE + g * DH : h * WIDE + (g + 1) * DH] for g in range(GROUP)], axis=0)
            scores.append(
                lax.dot_general(
                    jnp.concatenate([shards(0, h), k_marks], axis=1),
                    jnp.concatenate([q, q_marks], axis=1),
                    (((1,), (1,)), ((), ())),
                    preferred_element_type=jnp.float32,
                )
            )
    if kind == "end":
        m_lent, l_lent = lent_stats(lent)
        known = jnp.maximum(m_in[...], m_lent)
    tops, totals, weights = [], [], []
    for h in range(HK):
        if not some:
            tops.append(known[h : h + 1, :])
            continue
        top = jnp.max(scores[h], axis=0, keepdims=True)
        if kind == "end":
            top = jnp.maximum(top, known[h : h + 1, :])
        weight = jnp.exp2(scores[h] * RATE - top * RATE)
        tops.append(top)
        totals.append(jnp.sum(weight, axis=0, keepdims=True))
        weights.append(weight.astype(jnp.bfloat16))
    if kind == "lend":
        for i, (low, high) in enumerate(LOTS):
            pieces = in_three(jnp.concatenate(tops[low:high], axis=0)) + in_three(
                jnp.concatenate(totals[low:high], axis=0)
            )
            if STATS > 6 * (high - low):
                pieces += [jnp.zeros((STATS - 6 * (high - low), COLS), jnp.float32)]
            stats = jnp.concatenate(pieces, axis=0).astype(jnp.bfloat16)
            lent[i][(high - low) * DH : (high - low) * DH + STATS, :] = stats
    if kind == "own":
        m_out, l_out, acc_out = refs
        m_out[...] = jnp.concatenate(tops, axis=0)
        l_out[...] = jnp.concatenate(totals, axis=0)
    copies = []
    for h in range(HK):
        if some:
            part = lax.dot_general(
                shards(1, h), weights[h], (((0,), (0,)), ((), ())), preferred_element_type=jnp.float32
            )
        if kind == "own":
            acc_out[h] = part
        if kind == "lend":
            i, j = lot_of(h)
            lent[i][j * DH : (j + 1) * DH, :] = (part * (1.0 / totals[h])).astype(jnp.bfloat16)
        if kind == "end":
            i, j = lot_of(h)
            wide = slice(h * WIDE, (h + 1) * WIDE)
            held = jnp.exp2((m_in[h : h + 1, :] - tops[h]) * RATE)
            got = l_lent[h : h + 1, :] * jnp.exp2((m_lent[h : h + 1, :] - tops[h]) * RATE)
            total = l_in[h : h + 1, :] * held + got
            if some:
                total = total + totals[h]
            share = 1.0 / total
            result = acc_in[h] * (held * share)
            result = result + lent[i][j * DH : (j + 1) * DH, :].astype(jnp.float32) * (got * share)
            if some:
                result = result + part * share
            result = result.T.astype(jnp.bfloat16)
            for g in range(GROUP):
                staged[:, h * WIDE + g * DH : h * WIDE + (g + 1) * DH] = result[g * ROWS : (g + 1) * ROWS, :]
            copies.append(pltpu.make_async_copy(staged.at[:, wide], out_ref.at[:, wide], sems.at[h]))
            copies[-1].start()
    for copy in copies:
        copy.wait()


LOTS = ((0, 4), (4, 8))
STATS = 32
LENT = 640


def lot_of(h):
    for i, (low, high) in enumerate(LOTS):
        if low <= h < high:
            return i, h - low


def in_three(x):
    pieces = []
    for _ in range(3):
        pieces.append(x.astype(jnp.bfloat16).astype(jnp.float32))
        x = x - pieces[-1]
    return pieces


def lent_stats(lent):
    tops, totals = [], []
    for lot, (low, high) in zip(lent, LOTS):
        n = high - low
        stats = lot[n * DH : n * DH + STATS, :].astype(jnp.float32)
        pieces = [stats[i * n : (i + 1) * n, :] for i in range(6)]
        tops.append(pieces[0] + pieces[1] + pieces[2])
        totals.append(pieces[3] + pieces[4] + pieces[5])
    return jnp.concatenate(tops, axis=0), jnp.concatenate(totals, axis=0)


VMEM = pl.BlockSpec(memory_space=pltpu.VMEM)
SMEM = pl.BlockSpec(memory_space=pltpu.SMEM)
HBM = pl.BlockSpec(memory_space=pl.ANY)


def flash(kind, info, q, arrays, blocks, places):
    n = len(places)
    operands = [info, q] + list(arrays)
    in_specs = [SMEM] + [VMEM] * (len(operands) - 1)
    scratch = []
    out_specs = VMEM
    if kind == "end":
        out_shape = jax.ShapeDtypeStruct((ROWS, HQ * DH), jnp.bfloat16)
        out_specs = HBM
        scratch = [pltpu.VMEM((ROWS, HQ * DH), jnp.bfloat16), pltpu.SemaphoreType.DMA((HK,))]
    elif kind == "lend":
        out_specs = (VMEM,) * len(LOTS)
        out_shape = (jax.ShapeDtypeStruct((LENT, COLS), jnp.bfloat16),) * len(LOTS)
    else:
        out_specs = (VMEM, VMEM, VMEM)
        out_shape = (
            jax.ShapeDtypeStruct((HK, COLS), jnp.float32),
            jax.ShapeDtypeStruct((HK, COLS), jnp.float32),
            jax.ShapeDtypeStruct((HK, DH, COLS), jnp.float32),
        )
    return pl.pallas_call(
        functools.partial(flash_kernel, tuple(blocks), tuple(places), kind),
        out_shape=out_shape,
        in_specs=in_specs,
        out_specs=out_specs,
        scratch_shapes=scratch,
        compiler_params=pltpu.CompilerParams(vmem_limit_bytes=16 * 1024 * 1024),
        cost_estimate=pl.CostEstimate(
            flops=4 * n * ROWS * HQ * ROWS * DH, bytes_accessed=1 << 16, transcendentals=n * ROWS * HQ * ROWS
        ),
    )(*operands)


def per_device(queries, key_heads, value_heads, doc_lengths):
    here = lax.axis_index("seq").astype(jnp.int32).reshape(1)
    there = here + 1 - 2 * lax.rem(here, 2)
    info, info_there = (jnp.concatenate([place, doc_lengths]) for place in (here, there))

    def swap(block):
        return lax.ppermute(block, "seq", SIBLING)

    got = {0: jnp.concatenate([key_heads, value_heads], axis=0)}
    for chips, source in HOPS:
        got[chips] = lax.ppermute(got[source], "seq", chip_route(chips - source))
        if chips == HOPS[0][0]:
            got[chips], info, info_there = lax.optimization_barrier((got[chips], info, info_there))

    arrays = [got[c] for c in EARLY]
    blocks = [(i, 0) for i in range(len(EARLY))]
    lent = flash("lend", info_there, swap(queries), arrays, blocks, [(c, True) for c in EARLY])
    lent_here = [swap(x) for x in lent]
    q, _ = lax.optimization_barrier((queries, lent))
    state = flash("own", info, q, arrays, blocks, [(c, False) for c in EARLY])

    *mid, end = (got[c] for c in LATE)
    *mid, end, state = lax.optimization_barrier((*mid, end, state))
    arrays = mid + [end, swap(jnp.concatenate(mid, axis=0)), swap(end)]
    blocks = [(0, 0), (1, 0), (2, 0), (3, 0), (3, 2 * ROWS), (4, 0)]
    places = [(c, False) for c in LATE] + [(c, True) for c in LATE]
    return flash("end", info, queries, arrays + list(state) + lent_here, blocks, places)


def solution(mesh):
    return jax.shard_map(
        per_device,
        mesh=mesh,
        in_specs=(
            P(("grp", "seq"), None),
            P(("grp", "seq"), None),
            P(("grp", "seq"), None),
            P("grp"),
        ),
        out_specs=P(("grp", "seq"), None),
        check_vma=False,
    )
```

```python
import functools

import jax
import jax.numpy as jnp
from jax import lax
from jax.experimental import pallas as pl
from jax.experimental.pallas import tpu as pltpu
from jax.sharding import PartitionSpec as P

HK = 8
GROUP = 8
DH = 128
HQ = 64
ROWS = 64
DOCS = 8
COLS = GROUP * ROWS
WIDE = GROUP * DH
NEG = -1e30
RATE = DH ** (-0.5) * 1.4426950408889634

CHIPS = 32
NEAR = 4
FAR = 8


def chip_route(ahead):
    return [(2 * c + k, 2 * ((c + ahead) % CHIPS) + k) for c in range(CHIPS) for k in range(2)]


SIBLING = [(i, i ^ 1) for i in range(2 * CHIPS)]


def bands(info_ref):
    lane = lax.broadcasted_iota(jnp.int32, (ROWS, DH), 1)
    low = jnp.where(lane == ROWS + DOCS, -(1 << 30), 1 << 30)
    high = jnp.where(lane == ROWS + DOCS, 0, 1 << 30)
    end = jnp.int32(0)
    for d in range(DOCS):
        begin, end = end, end + info_ref[1 + d]
        low = jnp.where(lane == ROWS + d, begin, low)
        high = jnp.where(lane == ROWS + d, end, high)
    return lane, low, high


def query_marks(here, info_ref):
    lane, low, high = bands(info_ref)
    row = lax.broadcasted_iota(jnp.int32, (ROWS, DH), 0)
    pos = here * ROWS + row
    start = jnp.zeros_like(pos)
    end = jnp.int32(0)
    for d in range(DOCS):
        end = end + info_ref[1 + d]
        start = jnp.where(pos >= end, end, start)
    own = (lane <= row) & (here * ROWS + lane >= start)
    other = ((pos >= low) & (pos < high)) | (lane > ROWS + DOCS)
    marks = jnp.where(lane < ROWS, jnp.where(own, 0.0, NEG), jnp.where(other, 0.0, NEG))
    return marks.astype(jnp.bfloat16)


def key_marks(here, info_ref, places):
    lane, low, high = bands(info_ref)
    row = lax.broadcasted_iota(jnp.int32, (ROWS, DH), 0)
    core = lax.rem(here, 2)
    marks = []
    for chips, sibling in places:
        if chips == 0 and not sibling:
            hit = lane == row
        else:
            place = here - 2 * chips
            if sibling:
                place = place + 1 - 2 * core
            if chips == 0:
                place = jnp.where(core == 0, -1, place)
            pos = place * ROWS + row
            hit = (pos >= low) & (pos < high)
        marks.append(jnp.where(hit, 1.0, 0.0).astype(jnp.bfloat16))
    return jnp.concatenate(marks, axis=0)


def flash_kernel(places, kind, *refs):
    n = len(places)
    info_ref, q_ref = refs[:2]
    n_kv = 5 if kind == "end" else 2 * n - 1
    kv, refs = refs[2 : 2 + n_kv], refs[2 + n_kv :]

    here = info_ref[0]
    start = jnp.int32(0)
    end = jnp.int32(0)
    for d in range(DOCS):
        end = end + info_ref[1 + d]
        start = jnp.where(here * ROWS >= end, end, start)

    def reach(some):
        nearest = here - 2 * min(places[s][0] for s in some) + 1
        return nearest * ROWS + ROWS - 1 >= start

    base = [s for s in range(n) if places[s][0] == 0]
    near = [s for s in range(n) if 0 < places[s][0] <= NEAR]
    far = [s for s in range(n) if places[s][0] > NEAR]
    all_reach, near_reach = reach(far), reach(near)

    def attend(some):
        attend_some(some, places, kind, info_ref, q_ref, kv, refs)

    pl.when(all_reach)(lambda: attend(base + near + far))
    pl.when(near_reach & jnp.logical_not(all_reach))(lambda: attend(base + near))
    pl.when(jnp.logical_not(near_reach))(lambda: attend(base))


def attend_some(some, places, kind, info_ref, q_ref, kv, refs):
    here = info_ref[0]
    if kind == "lend":
        lent = refs
    if kind == "end":
        m_in, l_in, acc_in, *lent, out_ref, staged, sems = refs

    def shards(which, h):
        cols = slice(h * DH, (h + 1) * DH)
        parts = []
        for s in some:
            if kind == "end" and s >= 2:
                parts.append(kv[4][(2 * (s - 2) + which) * ROWS : (2 * (s - 2) + which + 1) * ROWS, cols])
            elif kind == "end":
                parts.append(kv[2 * s + which][:, cols])
            elif s == 0:
                parts.append(kv[0][which * ROWS : (which + 1) * ROWS, cols])
            else:
                parts.append(kv[2 * s - 1 + which][:, cols])
        return jnp.concatenate(parts, axis=0)

    scores = []
    if some:
        q_marks = jnp.concatenate([query_marks(here, info_ref)] * GROUP, axis=0)
        k_marks = key_marks(here, info_ref, [places[s] for s in some])
        for h in range(HK):
            q = jnp.concatenate([q_ref[:, h * WIDE + g * DH : h * WIDE + (g + 1) * DH] for g in range(GROUP)], axis=0)
            scores.append(
                lax.dot_general(
                    jnp.concatenate([shards(0, h), k_marks], axis=1),
                    jnp.concatenate([q, q_marks], axis=1),
                    (((1,), (1,)), ((), ())),
                    preferred_element_type=jnp.float32,
                )
            )
    if kind == "end":
        m_lent, l_lent = lent_stats(lent)
        known = jnp.maximum(m_in[...], m_lent)
    tops, totals, weights = [], [], []
    for h in range(HK):
        if not some:
            tops.append(known[h : h + 1, :])
            continue
        top = jnp.max(scores[h], axis=0, keepdims=True)
        if kind == "end":
            top = jnp.maximum(top, known[h : h + 1, :])
        weight = jnp.exp2((scores[h] - top) * RATE)
        tops.append(top)
        totals.append(jnp.sum(weight, axis=0, keepdims=True))
        weights.append(weight.astype(jnp.bfloat16))
    if kind == "lend":
        for i, (low, high) in enumerate(LOTS):
            pieces = in_three(jnp.concatenate(tops[low:high], axis=0)) + in_three(
                jnp.concatenate(totals[low:high], axis=0)
            )
            if STATS > 6 * (high - low):
                pieces += [jnp.zeros((STATS - 6 * (high - low), COLS), jnp.float32)]
            stats = jnp.concatenate(pieces, axis=0).astype(jnp.bfloat16)
            lent[i][(high - low) * DH : (high - low) * DH + STATS, :] = stats
    if kind == "own":
        m_out, l_out, acc_out = refs
        m_out[...] = jnp.concatenate(tops, axis=0)
        l_out[...] = jnp.concatenate(totals, axis=0)
    copies = []
    for h in range(HK):
        if some:
            part = lax.dot_general(
                shards(1, h), weights[h], (((0,), (0,)), ((), ())), preferred_element_type=jnp.float32
            )
        if kind == "own":
            acc_out[h] = part
        if kind == "lend":
            i, j = lot_of(h)
            lent[i][j * DH : (j + 1) * DH, :] = (part * (1.0 / totals[h])).astype(jnp.bfloat16)
        if kind == "end":
            i, j = lot_of(h)
            wide = slice(h * WIDE, (h + 1) * WIDE)
            held = jnp.exp2((m_in[h : h + 1, :] - tops[h]) * RATE)
            got = l_lent[h : h + 1, :] * jnp.exp2((m_lent[h : h + 1, :] - tops[h]) * RATE)
            total = l_in[h : h + 1, :] * held + got
            if some:
                total = total + totals[h]
            share = 1.0 / total
            result = acc_in[h] * (held * share)
            result = result + lent[i][j * DH : (j + 1) * DH, :].astype(jnp.float32) * (got * share)
            if some:
                result = result + part * share
            result = result.T.astype(jnp.bfloat16)
            for g in range(GROUP):
                staged[:, h * WIDE + g * DH : h * WIDE + (g + 1) * DH] = result[g * ROWS : (g + 1) * ROWS, :]
            copies.append(pltpu.make_async_copy(staged.at[:, wide], out_ref.at[:, wide], sems.at[h]))
            copies[-1].start()
    for copy in copies:
        copy.wait()


LOTS = ((0, 4), (4, 8))
STATS = 32
LENT = 640


def lot_of(h):
    for i, (low, high) in enumerate(LOTS):
        if low <= h < high:
            return i, h - low


def in_three(x):
    pieces = []
    for _ in range(3):
        pieces.append(x.astype(jnp.bfloat16).astype(jnp.float32))
        x = x - pieces[-1]
    return pieces


def lent_stats(lent):
    tops, totals = [], []
    for lot, (low, high) in zip(lent, LOTS):
        n = high - low
        stats = lot[n * DH : n * DH + STATS, :].astype(jnp.float32)
        pieces = [stats[i * n : (i + 1) * n, :] for i in range(6)]
        tops.append(pieces[0] + pieces[1] + pieces[2])
        totals.append(pieces[3] + pieces[4] + pieces[5])
    return jnp.concatenate(tops, axis=0), jnp.concatenate(totals, axis=0)


VMEM = pl.BlockSpec(memory_space=pltpu.VMEM)
SMEM = pl.BlockSpec(memory_space=pltpu.SMEM)
HBM = pl.BlockSpec(memory_space=pl.ANY)


def flash(kind, info, q, arrays, places):
    n = len(places)
    operands = [info, q] + list(arrays)
    in_specs = [SMEM] + [VMEM] * (len(operands) - 1)
    scratch = []
    out_specs = VMEM
    if kind == "end":
        out_shape = jax.ShapeDtypeStruct((ROWS, HQ * DH), jnp.bfloat16)
        out_specs = HBM
        scratch = [pltpu.VMEM((ROWS, HQ * DH), jnp.bfloat16), pltpu.SemaphoreType.DMA((HK,))]
    elif kind == "lend":
        out_specs = (VMEM,) * len(LOTS)
        out_shape = (jax.ShapeDtypeStruct((LENT, COLS), jnp.bfloat16),) * len(LOTS)
    else:
        out_specs = (VMEM, VMEM, VMEM)
        out_shape = (
            jax.ShapeDtypeStruct((HK, COLS), jnp.float32),
            jax.ShapeDtypeStruct((HK, COLS), jnp.float32),
            jax.ShapeDtypeStruct((HK, DH, COLS), jnp.float32),
        )
    return pl.pallas_call(
        functools.partial(flash_kernel, tuple(places), kind),
        out_shape=out_shape,
        in_specs=in_specs,
        out_specs=out_specs,
        scratch_shapes=scratch,
        compiler_params=pltpu.CompilerParams(vmem_limit_bytes=16 * 1024 * 1024),
        cost_estimate=pl.CostEstimate(
            flops=4 * n * ROWS * HQ * ROWS * DH, bytes_accessed=1 << 16, transcendentals=n * ROWS * HQ * ROWS
        ),
    )(*operands)


def per_device(queries, key_heads, value_heads, doc_lengths):
    here = lax.axis_index("seq").astype(jnp.int32).reshape(1)
    there = here + 1 - 2 * lax.rem(here, 2)
    info, info_there = (jnp.concatenate([place, doc_lengths]) for place in (here, there))

    def send(block, ahead):
        return lax.ppermute(block, "seq", chip_route(ahead))

    def swap(block):
        return lax.ppermute(block, "seq", SIBLING)

    own = (key_heads, value_heads)
    near, far = own, own
    shards = [jnp.concatenate(own, axis=0)]
    chips = [0]
    for step in range(NEAR):
        near = tuple(send(x, 1) for x in near)
        far = tuple(send(x, FAR if step == 0 else -1) for x in far)
        if step == 0:
            first, shards[0], info, info_there = lax.optimization_barrier((far[0], shards[0], info, info_there))
            far = (first, far[1])
        if step < NEAR - 1:
            shards += list(near + far)
            chips += [step + 1, FAR - step]
    end = near + far
    end_chips = [NEAR, FAR - NEAR + 1]

    lent = flash("lend", info_there, swap(queries), shards, [(c, True) for c in chips])
    got = [swap(x) for x in lent]
    q, _ = lax.optimization_barrier((queries, lent))
    state = flash("own", info, q, shards, [(c, False) for c in chips])
    end, state = lax.optimization_barrier((end, state))
    arrays = list(end) + [swap(jnp.concatenate(end, axis=0))] + list(state) + got
    places = [(c, False) for c in end_chips] + [(c, True) for c in end_chips]
    return flash("end", info, queries, arrays, places)


def solution(mesh):
    return jax.shard_map(
        per_device,
        mesh=mesh,
        in_specs=(
            P(("grp", "seq"), None),
            P(("grp", "seq"), None),
            P(("grp", "seq"), None),
            P("grp"),
        ),
        out_specs=P(("grp", "seq"), None),
        check_vma=False,
    )
```

```python
import functools

import jax
import jax.numpy as jnp
from jax import lax
from jax.experimental import pallas as pl
from jax.experimental.pallas import tpu as pltpu
from jax.sharding import PartitionSpec as P

HK = 8
GROUP = 8
DH = 128
HQ = 64
ROWS = 64
DOCS = 8
COLS = GROUP * ROWS
WIDE = GROUP * DH
NEG = -1e30
RATE = DH ** (-0.5) * 1.4426950408889634

CHIPS = 32
NEAR = 4
FAR = 8


def chip_route(ahead):
    return [(2 * c + k, 2 * ((c + ahead) % CHIPS) + k) for c in range(CHIPS) for k in range(2)]


SIBLING = [(i, i ^ 1) for i in range(2 * CHIPS)]


def bands(info_ref):
    lane = lax.broadcasted_iota(jnp.int32, (ROWS, DH), 1)
    low = jnp.where(lane == ROWS + DOCS, -(1 << 30), 1 << 30)
    high = jnp.where(lane == ROWS + DOCS, 0, 1 << 30)
    end = jnp.int32(0)
    for d in range(DOCS):
        begin, end = end, end + info_ref[1 + d]
        low = jnp.where(lane == ROWS + d, begin, low)
        high = jnp.where(lane == ROWS + d, end, high)
    return lane, low, high


def query_marks(here, info_ref):
    lane, low, high = bands(info_ref)
    row = lax.broadcasted_iota(jnp.int32, (ROWS, DH), 0)
    pos = here * ROWS + row
    start = jnp.zeros_like(pos)
    end = jnp.int32(0)
    for d in range(DOCS):
        end = end + info_ref[1 + d]
        start = jnp.where(pos >= end, end, start)
    own = (lane <= row) & (here * ROWS + lane >= start)
    other = ((pos >= low) & (pos < high)) | (lane > ROWS + DOCS)
    marks = jnp.where(lane < ROWS, jnp.where(own, 0.0, NEG), jnp.where(other, 0.0, NEG))
    return marks.astype(jnp.bfloat16)


def key_marks(here, info_ref, places):
    lane, low, high = bands(info_ref)
    row = lax.broadcasted_iota(jnp.int32, (ROWS, DH), 0)
    core = lax.rem(here, 2)
    marks = []
    for chips, sibling in places:
        if chips == 0 and not sibling:
            hit = lane == row
        else:
            place = here - 2 * chips
            if sibling:
                place = place + 1 - 2 * core
            if chips == 0:
                place = jnp.where(core == 0, -1, place)
            pos = place * ROWS + row
            hit = (pos >= low) & (pos < high)
        marks.append(jnp.where(hit, 1.0, 0.0).astype(jnp.bfloat16))
    return jnp.concatenate(marks, axis=0)


def flash_kernel(places, kind, *refs):
    n = len(places)
    info_ref, q_ref = refs[:2]
    n_kv = 5 if kind == "end" else 2 * n - 1
    kv, refs = refs[2 : 2 + n_kv], refs[2 + n_kv :]

    here = info_ref[0]
    start = jnp.int32(0)
    end = jnp.int32(0)
    for d in range(DOCS):
        end = end + info_ref[1 + d]
        start = jnp.where(here * ROWS >= end, end, start)

    def reach(some):
        core = lax.rem(here, 2)
        ahead = {"end": 1 - core, "lend": 1 - 2 * core, "own": 0}[kind]
        nearest = here - 2 * min(places[s][0] for s in some) + ahead
        return nearest * ROWS + ROWS - 1 >= start

    base = [s for s in range(n) if places[s][0] == 0]
    near = [s for s in range(n) if 0 < places[s][0] <= NEAR]
    far = [s for s in range(n) if places[s][0] > NEAR]
    all_reach, near_reach = reach(far), reach(near)

    def attend(some):
        attend_some(some, places, kind, info_ref, q_ref, kv, refs)

    pl.when(all_reach)(lambda: attend(base + near + far))
    pl.when(near_reach & jnp.logical_not(all_reach))(lambda: attend(base + near))
    pl.when(jnp.logical_not(near_reach))(lambda: attend(base))


def attend_some(some, places, kind, info_ref, q_ref, kv, refs):
    here = info_ref[0]
    if kind == "lend":
        lent = refs
    if kind == "end":
        m_in, l_in, acc_in, *lent, out_ref, staged, sems = refs

    def shards(which, h):
        cols = slice(h * DH, (h + 1) * DH)
        parts = []
        for s in some:
            if kind == "end" and s >= 2:
                parts.append(kv[4][(2 * (s - 2) + which) * ROWS : (2 * (s - 2) + which + 1) * ROWS, cols])
            elif kind == "end":
                parts.append(kv[2 * s + which][:, cols])
            elif s == 0:
                parts.append(kv[0][which * ROWS : (which + 1) * ROWS, cols])
            else:
                parts.append(kv[2 * s - 1 + which][:, cols])
        return jnp.concatenate(parts, axis=0)

    scores = []
    if some:
        q_marks = jnp.concatenate([query_marks(here, info_ref)] * GROUP, axis=0)
        k_marks = key_marks(here, info_ref, [places[s] for s in some])
        for h in range(HK):
            q = jnp.concatenate([q_ref[:, h * WIDE + g * DH : h * WIDE + (g + 1) * DH] for g in range(GROUP)], axis=0)
            scores.append(
                lax.dot_general(
                    jnp.concatenate([shards(0, h), k_marks], axis=1),
                    jnp.concatenate([q, q_marks], axis=1),
                    (((1,), (1,)), ((), ())),
                    preferred_element_type=jnp.float32,
                )
            )
    if kind == "end":
        m_lent, l_lent = lent_stats(lent)
        known = jnp.maximum(m_in[...], m_lent)
    tops, totals, weights = [], [], []
    for h in range(HK):
        if not some:
            tops.append(known[h : h + 1, :])
            continue
        top = jnp.max(scores[h], axis=0, keepdims=True)
        if kind == "end":
            top = jnp.maximum(top, known[h : h + 1, :])
        weight = jnp.exp2((scores[h] - top) * RATE)
        tops.append(top)
        totals.append(jnp.sum(weight, axis=0, keepdims=True))
        weights.append(weight.astype(jnp.bfloat16))
    if kind == "lend":
        for i, (low, high) in enumerate(LOTS):
            pieces = in_three(jnp.concatenate(tops[low:high], axis=0)) + in_three(
                jnp.concatenate(totals[low:high], axis=0)
            )
            if STATS > 6 * (high - low):
                pieces += [jnp.zeros((STATS - 6 * (high - low), COLS), jnp.float32)]
            stats = jnp.concatenate(pieces, axis=0).astype(jnp.bfloat16)
            lent[i][(high - low) * DH : (high - low) * DH + STATS, :] = stats
    if kind == "own":
        m_out, l_out, acc_out = refs
        m_out[...] = jnp.concatenate(tops, axis=0)
        l_out[...] = jnp.concatenate(totals, axis=0)
    copies = []
    for h in range(HK):
        if some:
            part = lax.dot_general(
                shards(1, h), weights[h], (((0,), (0,)), ((), ())), preferred_element_type=jnp.float32
            )
        if kind == "own":
            acc_out[h] = part
        if kind == "lend":
            i, j = lot_of(h)
            lent[i][j * DH : (j + 1) * DH, :] = (part * (1.0 / totals[h])).astype(jnp.bfloat16)
        if kind == "end":
            i, j = lot_of(h)
            wide = slice(h * WIDE, (h + 1) * WIDE)
            held = jnp.exp2((m_in[h : h + 1, :] - tops[h]) * RATE)
            got = l_lent[h : h + 1, :] * jnp.exp2((m_lent[h : h + 1, :] - tops[h]) * RATE)
            total = l_in[h : h + 1, :] * held + got
            if some:
                total = total + totals[h]
            share = 1.0 / total
            result = acc_in[h] * (held * share)
            result = result + lent[i][j * DH : (j + 1) * DH, :].astype(jnp.float32) * (got * share)
            if some:
                result = result + part * share
            result = result.T.astype(jnp.bfloat16)
            for g in range(GROUP):
                staged[:, h * WIDE + g * DH : h * WIDE + (g + 1) * DH] = result[g * ROWS : (g + 1) * ROWS, :]
            copies.append(pltpu.make_async_copy(staged.at[:, wide], out_ref.at[:, wide], sems.at[h]))
            copies[-1].start()
    for copy in copies:
        copy.wait()


LOTS = ((0, 4), (4, 8))
STATS = 32
LENT = 640


def lot_of(h):
    for i, (low, high) in enumerate(LOTS):
        if low <= h < high:
            return i, h - low


def in_three(x):
    pieces = []
    for _ in range(3):
        pieces.append(x.astype(jnp.bfloat16).astype(jnp.float32))
        x = x - pieces[-1]
    return pieces


def lent_stats(lent):
    tops, totals = [], []
    for lot, (low, high) in zip(lent, LOTS):
        n = high - low
        stats = lot[n * DH : n * DH + STATS, :].astype(jnp.float32)
        pieces = [stats[i * n : (i + 1) * n, :] for i in range(6)]
        tops.append(pieces[0] + pieces[1] + pieces[2])
        totals.append(pieces[3] + pieces[4] + pieces[5])
    return jnp.concatenate(tops, axis=0), jnp.concatenate(totals, axis=0)


VMEM = pl.BlockSpec(memory_space=pltpu.VMEM)
SMEM = pl.BlockSpec(memory_space=pltpu.SMEM)
HBM = pl.BlockSpec(memory_space=pl.ANY)


def flash(kind, info, q, arrays, places):
    n = len(places)
    operands = [info, q] + list(arrays)
    in_specs = [SMEM] + [VMEM] * (len(operands) - 1)
    scratch = []
    out_specs = VMEM
    if kind == "end":
        out_shape = jax.ShapeDtypeStruct((ROWS, HQ * DH), jnp.bfloat16)
        out_specs = HBM
        scratch = [pltpu.VMEM((ROWS, HQ * DH), jnp.bfloat16), pltpu.SemaphoreType.DMA((HK,))]
    elif kind == "lend":
        out_specs = (VMEM,) * len(LOTS)
        out_shape = (jax.ShapeDtypeStruct((LENT, COLS), jnp.bfloat16),) * len(LOTS)
    else:
        out_specs = (VMEM, VMEM, VMEM)
        out_shape = (
            jax.ShapeDtypeStruct((HK, COLS), jnp.float32),
            jax.ShapeDtypeStruct((HK, COLS), jnp.float32),
            jax.ShapeDtypeStruct((HK, DH, COLS), jnp.float32),
        )
    return pl.pallas_call(
        functools.partial(flash_kernel, tuple(places), kind),
        out_shape=out_shape,
        in_specs=in_specs,
        out_specs=out_specs,
        scratch_shapes=scratch,
        compiler_params=pltpu.CompilerParams(vmem_limit_bytes=16 * 1024 * 1024),
        cost_estimate=pl.CostEstimate(
            flops=4 * n * ROWS * HQ * ROWS * DH, bytes_accessed=1 << 16, transcendentals=n * ROWS * HQ * ROWS
        ),
    )(*operands)


def per_device(queries, key_heads, value_heads, doc_lengths):
    here = lax.axis_index("seq").astype(jnp.int32).reshape(1)
    there = here + 1 - 2 * lax.rem(here, 2)
    info, info_there = (jnp.concatenate([place, doc_lengths]) for place in (here, there))

    def send(block, ahead):
        return lax.ppermute(block, "seq", chip_route(ahead))

    def swap(block):
        return lax.ppermute(block, "seq", SIBLING)

    own = (key_heads, value_heads)
    near, far = own, own
    shards = [jnp.concatenate(own, axis=0)]
    chips = [0]
    for step in range(NEAR):
        near = tuple(send(x, 1) for x in near)
        far = tuple(send(x, FAR if step == 0 else -1) for x in far)
        if step == 0:
            first, shards[0], info, info_there = lax.optimization_barrier((far[0], shards[0], info, info_there))
            far = (first, far[1])
        if step < NEAR - 1:
            shards += list(near + far)
            chips += [step + 1, FAR - step]
    end = near + far
    end_chips = [NEAR, FAR - NEAR + 1]

    lent = flash("lend", info_there, swap(queries), shards, [(c, True) for c in chips])
    got = [swap(x) for x in lent]
    q, _ = lax.optimization_barrier((queries, lent))
    state = flash("own", info, q, shards, [(c, False) for c in chips])
    end, state = lax.optimization_barrier((end, state))
    arrays = list(end) + [swap(jnp.concatenate(end, axis=0))] + list(state) + got
    places = [(c, False) for c in end_chips] + [(c, True) for c in end_chips]
    return flash("end", info, queries, arrays, places)


def solution(mesh):
    return jax.shard_map(
        per_device,
        mesh=mesh,
        in_specs=(
            P(("grp", "seq"), None),
            P(("grp", "seq"), None),
            P(("grp", "seq"), None),
            P("grp"),
        ),
        out_specs=P(("grp", "seq"), None),
        check_vma=False,
    )
```

```python
import functools

import jax
import jax.numpy as jnp
from jax import lax
from jax.experimental import pallas as pl
from jax.experimental.pallas import tpu as pltpu
from jax.sharding import PartitionSpec as P

HK = 8
GROUP = 8
DH = 128
HQ = 64
ROWS = 64
DOCS = 8
COLS = GROUP * ROWS
WIDE = GROUP * DH
NEG = -1e30
RATE = DH ** (-0.5) * 1.4426950408889634

CHIPS = 32
NEAR = 4
FAR = 8


def chip_route(ahead):
    return [(2 * c + k, 2 * ((c + ahead) % CHIPS) + k) for c in range(CHIPS) for k in range(2)]


SIBLING = [(i, i ^ 1) for i in range(2 * CHIPS)]


def bands(info_ref):
    lane = lax.broadcasted_iota(jnp.int32, (ROWS, DH), 1)
    low = jnp.where(lane == ROWS + DOCS, -(1 << 30), 1 << 30)
    high = jnp.where(lane == ROWS + DOCS, 0, 1 << 30)
    end = jnp.int32(0)
    for d in range(DOCS):
        begin, end = end, end + info_ref[1 + d]
        low = jnp.where(lane == ROWS + d, begin, low)
        high = jnp.where(lane == ROWS + d, end, high)
    return lane, low, high


def query_marks(here, info_ref):
    lane, low, high = bands(info_ref)
    row = lax.broadcasted_iota(jnp.int32, (ROWS, DH), 0)
    pos = here * ROWS + row
    start = jnp.zeros_like(pos)
    end = jnp.int32(0)
    for d in range(DOCS):
        end = end + info_ref[1 + d]
        start = jnp.where(pos >= end, end, start)
    own = (lane <= row) & (here * ROWS + lane >= start)
    other = ((pos >= low) & (pos < high)) | (lane > ROWS + DOCS)
    marks = jnp.where(lane < ROWS, jnp.where(own, 0.0, NEG), jnp.where(other, 0.0, NEG))
    return marks.astype(jnp.bfloat16)


def key_marks(here, info_ref, places):
    lane, low, high = bands(info_ref)
    row = lax.broadcasted_iota(jnp.int32, (ROWS, DH), 0)
    core = lax.rem(here, 2)
    marks = []
    for chips, sibling in places:
        if chips == 0 and not sibling:
            hit = lane == row
        else:
            place = here - 2 * chips
            if sibling:
                place = place + 1 - 2 * core
            if chips == 0:
                place = jnp.where(core == 0, -1, place)
            pos = place * ROWS + row
            hit = (pos >= low) & (pos < high)
        marks.append(jnp.where(hit, 1.0, 0.0).astype(jnp.bfloat16))
    return jnp.concatenate(marks, axis=0)


def flash_kernel(places, kind, *refs):
    n = len(places)
    info_ref, q_ref = refs[:2]
    n_kv = 5 if kind == "end" else 2 * n - 1
    kv, refs = refs[2 : 2 + n_kv], refs[2 + n_kv :]

    here = info_ref[0]
    start = jnp.int32(0)
    end = jnp.int32(0)
    for d in range(DOCS):
        end = end + info_ref[1 + d]
        start = jnp.where(here * ROWS >= end, end, start)

    def reach(some):
        nearest = here - 2 * min(places[s][0] for s in some) + 1
        return nearest * ROWS + ROWS - 1 >= start

    base = [s for s in range(n) if places[s][0] == 0]
    near = [s for s in range(n) if 0 < places[s][0] <= NEAR]
    far = [s for s in range(n) if places[s][0] > NEAR]
    all_reach, near_reach = reach(far), reach(near)

    def attend(some):
        attend_some(some, places, kind, info_ref, q_ref, kv, refs)

    pl.when(all_reach)(lambda: attend(base + near + far))
    pl.when(near_reach & jnp.logical_not(all_reach))(lambda: attend(base + near))
    pl.when(jnp.logical_not(near_reach))(lambda: attend(base))


def attend_some(some, places, kind, info_ref, q_ref, kv, refs):
    here = info_ref[0]
    if kind == "lend":
        lent = refs
    if kind == "end":
        m_in, l_in, acc_in, *lent, out_ref, staged, sems = refs

    def shards(which, h):
        cols = slice(h * DH, (h + 1) * DH)
        parts = []
        for s in some:
            if kind == "end" and s >= 2:
                parts.append(kv[4][(2 * (s - 2) + which) * ROWS : (2 * (s - 2) + which + 1) * ROWS, cols])
            elif kind == "end":
                parts.append(kv[2 * s + which][:, cols])
            elif s == 0:
                parts.append(kv[0][which * ROWS : (which + 1) * ROWS, cols])
            else:
                parts.append(kv[2 * s - 1 + which][:, cols])
        return jnp.concatenate(parts, axis=0)

    scores = []
    if some:
        q_marks = jnp.concatenate([query_marks(here, info_ref)] * GROUP, axis=0)
        k_marks = key_marks(here, info_ref, [places[s] for s in some])
        for h in range(HK):
            q = jnp.concatenate([q_ref[:, h * WIDE + g * DH : h * WIDE + (g + 1) * DH] for g in range(GROUP)], axis=0)
            scores.append(
                lax.dot_general(
                    jnp.concatenate([shards(0, h), k_marks], axis=1),
                    jnp.concatenate([q, q_marks], axis=1),
                    (((1,), (1,)), ((), ())),
                    preferred_element_type=jnp.float32,
                )
            )
    if kind == "end":
        m_lent, l_lent = lent_stats(lent)
        known = jnp.maximum(m_in[...], m_lent)
    tops, totals, weights = [], [], []
    for h in range(HK):
        if not some:
            tops.append(known[h : h + 1, :])
            continue
        top = jnp.max(scores[h], axis=0, keepdims=True)
        if kind == "end":
            top = jnp.maximum(top, known[h : h + 1, :])
        weight = jnp.exp2((scores[h] - top) * RATE)
        tops.append(top)
        totals.append(jnp.sum(weight, axis=0, keepdims=True))
        weights.append(weight.astype(jnp.bfloat16))
    if kind == "lend":
        for i, (low, high) in enumerate(LOTS):
            pieces = in_three(jnp.concatenate(tops[low:high], axis=0)) + in_three(
                jnp.concatenate(totals[low:high], axis=0)
            )
            if STATS > 6 * (high - low):
                pieces += [jnp.zeros((STATS - 6 * (high - low), COLS), jnp.float32)]
            stats = jnp.concatenate(pieces, axis=0).astype(jnp.bfloat16)
            lent[i][(high - low) * DH : (high - low) * DH + STATS, :] = stats
    if kind == "own":
        m_out, l_out, acc_out = refs
        m_out[...] = jnp.concatenate(tops, axis=0)
        l_out[...] = jnp.concatenate(totals, axis=0)
    copies = []
    for h in range(HK):
        if some:
            part = lax.dot_general(
                shards(1, h), weights[h], (((0,), (0,)), ((), ())), preferred_element_type=jnp.float32
            )
        if kind == "own":
            acc_out[h] = part
        if kind == "lend":
            i, j = lot_of(h)
            lent[i][j * DH : (j + 1) * DH, :] = (part * (1.0 / totals[h])).astype(jnp.bfloat16)
        if kind == "end":
            i, j = lot_of(h)
            wide = slice(h * WIDE, (h + 1) * WIDE)
            held = jnp.exp2((m_in[h : h + 1, :] - tops[h]) * RATE)
            got = l_lent[h : h + 1, :] * jnp.exp2((m_lent[h : h + 1, :] - tops[h]) * RATE)
            total = l_in[h : h + 1, :] * held + got
            if some:
                total = total + totals[h]
            share = 1.0 / total
            result = acc_in[h] * (held * share)
            result = result + lent[i][j * DH : (j + 1) * DH, :].astype(jnp.float32) * (got * share)
            if some:
                result = result + part * share
            result = result.T.astype(jnp.bfloat16) if some else result.astype(jnp.bfloat16).T
            for g in range(GROUP):
                staged[:, h * WIDE + g * DH : h * WIDE + (g + 1) * DH] = result[g * ROWS : (g + 1) * ROWS, :]
            copies.append(pltpu.make_async_copy(staged.at[:, wide], out_ref.at[:, wide], sems.at[h]))
            copies[-1].start()
    for copy in copies:
        copy.wait()


LOTS = ((0, 4), (4, 8))
STATS = 32
LENT = 640


def lot_of(h):
    for i, (low, high) in enumerate(LOTS):
        if low <= h < high:
            return i, h - low


def in_three(x):
    pieces = []
    for _ in range(3):
        pieces.append(x.astype(jnp.bfloat16).astype(jnp.float32))
        x = x - pieces[-1]
    return pieces


def lent_stats(lent):
    tops, totals = [], []
    for lot, (low, high) in zip(lent, LOTS):
        n = high - low
        stats = lot[n * DH : n * DH + STATS, :].astype(jnp.float32)
        pieces = [stats[i * n : (i + 1) * n, :] for i in range(6)]
        tops.append(pieces[0] + pieces[1] + pieces[2])
        totals.append(pieces[3] + pieces[4] + pieces[5])
    return jnp.concatenate(tops, axis=0), jnp.concatenate(totals, axis=0)


VMEM = pl.BlockSpec(memory_space=pltpu.VMEM)
SMEM = pl.BlockSpec(memory_space=pltpu.SMEM)
HBM = pl.BlockSpec(memory_space=pl.ANY)


def flash(kind, info, q, arrays, places):
    n = len(places)
    operands = [info, q] + list(arrays)
    in_specs = [SMEM] + [VMEM] * (len(operands) - 1)
    scratch = []
    out_specs = VMEM
    if kind == "end":
        out_shape = jax.ShapeDtypeStruct((ROWS, HQ * DH), jnp.bfloat16)
        out_specs = HBM
        scratch = [pltpu.VMEM((ROWS, HQ * DH), jnp.bfloat16), pltpu.SemaphoreType.DMA((HK,))]
    elif kind == "lend":
        out_specs = (VMEM,) * len(LOTS)
        out_shape = (jax.ShapeDtypeStruct((LENT, COLS), jnp.bfloat16),) * len(LOTS)
    else:
        out_specs = (VMEM, VMEM, VMEM)
        out_shape = (
            jax.ShapeDtypeStruct((HK, COLS), jnp.float32),
            jax.ShapeDtypeStruct((HK, COLS), jnp.float32),
            jax.ShapeDtypeStruct((HK, DH, COLS), jnp.float32),
        )
    return pl.pallas_call(
        functools.partial(flash_kernel, tuple(places), kind),
        out_shape=out_shape,
        in_specs=in_specs,
        out_specs=out_specs,
        scratch_shapes=scratch,
        compiler_params=pltpu.CompilerParams(vmem_limit_bytes=16 * 1024 * 1024),
        cost_estimate=pl.CostEstimate(
            flops=4 * n * ROWS * HQ * ROWS * DH, bytes_accessed=1 << 16, transcendentals=n * ROWS * HQ * ROWS
        ),
    )(*operands)


def per_device(queries, key_heads, value_heads, doc_lengths):
    here = lax.axis_index("seq").astype(jnp.int32).reshape(1)
    there = here + 1 - 2 * lax.rem(here, 2)
    info, info_there = (jnp.concatenate([place, doc_lengths]) for place in (here, there))

    def send(block, ahead):
        return lax.ppermute(block, "seq", chip_route(ahead))

    def swap(block):
        return lax.ppermute(block, "seq", SIBLING)

    own = (key_heads, value_heads)
    near, far = own, own
    shards = [jnp.concatenate(own, axis=0)]
    chips = [0]
    for step in range(NEAR):
        near = tuple(send(x, 1) for x in near)
        far = tuple(send(x, FAR if step == 0 else -1) for x in far)
        if step == 0:
            first, shards[0], info, info_there = lax.optimization_barrier((far[0], shards[0], info, info_there))
            far = (first, far[1])
        if step < NEAR - 1:
            shards += list(near + far)
            chips += [step + 1, FAR - step]
    end = near + far
    end_chips = [NEAR, FAR - NEAR + 1]

    lent = flash("lend", info_there, swap(queries), shards, [(c, True) for c in chips])
    got = [swap(x) for x in lent]
    q, _ = lax.optimization_barrier((queries, lent))
    state = flash("own", info, q, shards, [(c, False) for c in chips])
    end, state = lax.optimization_barrier((end, state))
    arrays = list(end) + [swap(jnp.concatenate(end, axis=0))] + list(state) + got
    places = [(c, False) for c in end_chips] + [(c, True) for c in end_chips]
    return flash("end", info, queries, arrays, places)


def solution(mesh):
    return jax.shard_map(
        per_device,
        mesh=mesh,
        in_specs=(
            P(("grp", "seq"), None),
            P(("grp", "seq"), None),
            P(("grp", "seq"), None),
            P("grp"),
        ),
        out_specs=P(("grp", "seq"), None),
        check_vma=False,
    )
```
